32 devices in a mesh: pipe: 8 (over z, y), expert: 4 (over x, core).
Axes of the slice: x: 2, y: 2, z: 4, core: 2. Of those that a mesh axis runs over, the one named last changes fastest.
Arguments:
- section_in_a: bfloat16 [8, 512, 4096], P('pipe', 'expert'), may hold values from -6 to 6
- route_a: int32 [8, 512, 8], P('pipe', 'expert'), may hold values from 0 to 127, as said below
- router: bfloat16 [8, 4096, 128], P('pipe'), may hold values from -0.09375 to 0.09375
- gate_up: bfloat16 [8, 2, 4096, 1024], P('pipe', None, None, 'expert'), may hold values from -0.09375 to 0.09375
- down_proj: bfloat16 [8, 1024, 4096], P('pipe', 'expert'), may hold values from -1 to 1
- section_in_b: bfloat16 [8, 512, 4096], P('pipe', 'expert'), may hold values from -6 to 6
- route_b: int32 [8, 512, 8], P('pipe', 'expert'), may hold values from 0 to 127, as said below
- grad_out_b: bfloat16 [8, 512, 4096], P('pipe', 'expert'), may hold values from -6 to 6
Outputs:
- section_out_a: bfloat16 [8, 512, 4096], P('pipe', 'expert')
- grad_in_b: bfloat16 [8, 512, 4096], P('pipe', 'expert')
- grad_gate_up: bfloat16 [8, 2, 4096, 1024], P('pipe', None, None, 'expert')
- grad_down: bfloat16 [8, 1024, 4096], P('pipe', 'expert')
- grad_router: bfloat16 [8, 4096, 128], P('pipe', 'expert')
The draws below stay inside these ranges and needn't reach their ends.
Inputs may be any that keep to these rules, and one draw needn't show every extreme that they name: `route_a`: each row names 8 different experts in no particular order. Of the 128 rows of one device, at most 16 name any one expert below 1; for each such expert some section has every device's rows name it exactly 16 times. `route_b`: as for route_a.
All inputs are finite; a program needn't handle non-finite values.
Results may differ from the reference program's by a relative error of at most 0.0095.
Values may be sent and summed in bfloat16 or wider, within the bound.
No kernel may reach another device: no remote copies, remote signals or barrier semaphores. Data moves between devices by JAX's collectives and lax.ppermute only.
A program may use at most 128 MiB of HBM per device.

```python
import jax
import jax.numpy as jnp
from jax import lax

D = 4096
EXPERTS = 128
TOPK = 8
FF = 1024
TOK_DEV = 128
WSPLIT = 4
FF_DEV = 256
FLIGHT = 1
CAP = 16
TOKENS = 512
N_PIPE = 8


def route_draw(key):
    blocks = TOKENS // TOK_DEV
    subkeys = jax.random.split(key, 5)
    counts = jax.random.randint(subkeys[0], (N_PIPE, blocks, FLIGHT), CAP // 4, CAP + 1)
    full_section = jax.random.randint(subkeys[1], (FLIGHT,), 0, N_PIPE)
    section_ids = jnp.arange(N_PIPE)[:, None, None]
    counts = jnp.where(section_ids == full_section[None, None, :], CAP, counts)
    order_keys = jax.random.randint(subkeys[2], (N_PIPE, blocks, FLIGHT, TOK_DEV), 0, 2 ** 20) * TOK_DEV + jnp.arange(TOK_DEV)
    order_rank = jnp.argsort(jnp.argsort(order_keys, axis=-1), axis=-1)
    chosen = order_rank < counts[..., None]
    chosen = jnp.transpose(chosen, (0, 1, 3, 2)).reshape(N_PIPE, TOKENS, FLIGHT)
    others = jax.random.randint(subkeys[3], (N_PIPE, TOKENS, EXPERTS - FLIGHT), 0, 2 ** 16) * EXPERTS + jnp.arange(EXPERTS - FLIGHT)
    flight_scores = jnp.where(chosen, 2 ** 30 + jnp.arange(FLIGHT), -1)
    scores = jnp.concatenate([flight_scores, others], axis=-1)
    ranked = lax.top_k(scores, TOPK)[1]
    mixing = jax.random.randint(subkeys[4], (N_PIPE, TOKENS, TOPK), 0, 2 ** 20) * TOPK + jnp.arange(TOPK)
    return jnp.take_along_axis(ranked, jnp.argsort(mixing, axis=-1), axis=-1).astype(jnp.int32)


def draw_route_a(key, part):
    key = jax.random.fold_in(key, 11)
    return route_draw(key)


def draw_route_b(key, part):
    key = jax.random.fold_in(key, 23)
    return route_draw(key)


def block_scale(own_key, shape, pieces, smallest, high):
    level, own = 1.0, jax.random.fold_in(own_key, 6)
    for position, blocks in pieces:
        heights = jnp.exp(jax.random.uniform(jax.random.fold_in(own, position), (blocks,), jnp.float32, smallest / len(pieces), high / len(pieces)))
        level = level * jnp.repeat(heights, shape[position] // blocks).reshape([-1 if axis == position else 1 for axis in range(len(shape))])
    return level


def noise(key, shape, spread, reach, pieces=(), held_as=jnp.bfloat16):
    values = spread * jax.random.normal(key, shape, jnp.float32)
    if pieces:
        values = values * block_scale(key, shape, pieces, -0.22, 0.18)
    return jnp.clip(values, -reach, reach).astype(held_as)


def setup_inputs(seed: int = 0) -> dict:
    streams_of = jax.random.split(jax.random.key(seed), 9)
    section_in_a = noise(streams_of[0], (N_PIPE, TOKENS, D), 1.0, 6.0, ((0, 8), (1, 4)))
    route_a = draw_route_a(jax.random.fold_in(streams_of[8], 71), 0)
    router = noise(streams_of[2], (N_PIPE, D, EXPERTS), D ** -0.5, 0.09375, ((0, 8),))
    gate_up = noise(streams_of[3], (N_PIPE, 2, D, FLIGHT * FF), D ** -0.5, 0.09375, ((0, 8), (3, 4)))
    down_proj = noise(streams_of[4], (N_PIPE, FLIGHT * FF, D), (FF // 32) ** -0.5, 1.0, ((0, 8), (1, 4)))
    section_in_b = noise(streams_of[5], (N_PIPE, TOKENS, D), 1.0, 6.0, ((0, 8), (1, 4)))
    route_b = draw_route_b(jax.random.fold_in(streams_of[8], 71), 0)
    grad_out_b = noise(streams_of[7], (N_PIPE, TOKENS, D), 1.0, 6.0, ((0, 8), (1, 4)))
    return {"section_in_a": section_in_a, "route_a": route_a, "router": router, "gate_up": gate_up, "down_proj": down_proj, "section_in_b": section_in_b, "route_b": route_b, "grad_out_b": grad_out_b}


best_precision = lax.Precision.HIGHEST


def slot_tables(expert_ids):
    blocks = TOKENS // TOK_DEV
    named_mask = jnp.stack([jnp.any(expert_ids == expert_id, axis=1) for expert_id in range(FLIGHT)]).astype(jnp.int32)
    named_mask = named_mask.reshape(FLIGHT, blocks, TOK_DEV)
    order_rank = jnp.cumsum(named_mask, axis=2) - named_mask
    slot_ids = jnp.arange(CAP, dtype=jnp.int32)
    select = (named_mask[:, :, None, :] == 1) & (order_rank[:, :, None, :] == slot_ids[None, None, :, None])
    return select.astype(jnp.float32)


def gating(tokens_in, expert_ids, router_table):
    logits = jnp.dot(tokens_in, router_table, preferred_element_type=jnp.float32)
    onehot = (expert_ids[:, :, None] == jnp.arange(EXPERTS, dtype=jnp.int32)[None, None, :]).astype(jnp.float32)
    chosen = jnp.sum(onehot * logits[:, None, :], axis=2)
    gate_prob = jax.nn.softmax(chosen, axis=-1)
    weights = jnp.stack([jnp.sum(gate_prob * (expert_ids == expert_id).astype(jnp.float32), axis=1) for expert_id in range(FLIGHT)], axis=1)
    return onehot, gate_prob, weights.astype(jnp.bfloat16)


def pick_rows(select_one, values):
    blocks = select_one.shape[0]
    picked = jnp.einsum('bst,btd->bsd', select_one, values.astype(jnp.float32).reshape(blocks, TOK_DEV, -1), precision=best_precision)
    return picked.reshape(blocks * CAP, -1)


def shard_sum(products):
    rounded = lax.optimization_barrier(products.astype(jnp.bfloat16))
    return jnp.sum(rounded.astype(jnp.float32), axis=1)


def expert_parts(gathered, w_gate, w_up, w_down):
    act_gate = jnp.dot(gathered, w_gate, preferred_element_type=jnp.float32)
    act_up = jnp.dot(gathered, w_up, preferred_element_type=jnp.float32)
    hidden = (jax.nn.silu(act_gate) * act_up).astype(jnp.bfloat16)
    row_count = gathered.shape[0]
    products = jnp.einsum('rwk,wkd->rwd', hidden.astype(jnp.float32).reshape(row_count, WSPLIT, FF_DEV),
                          w_down.astype(jnp.float32).reshape(WSPLIT, FF_DEV, D), precision=best_precision)
    return act_gate, act_up, hidden, shard_sum(products)


def forward_section(tokens_in, expert_ids, router_table, gate_up, down_proj):
    select = slot_tables(expert_ids)
    onehot, gate_prob, weights = gating(tokens_in, expert_ids, router_table)
    blocks = select.shape[1]
    update = jnp.zeros((blocks, TOK_DEV, D), jnp.float32)
    for expert_id in range(FLIGHT):
        first_col = expert_id * FF
        last_col = first_col + FF
        gathered = pick_rows(select[expert_id], tokens_in).astype(jnp.bfloat16)
        expert_out = expert_parts(gathered, gate_up[0][:, first_col:last_col], gate_up[1][:, first_col:last_col], down_proj[first_col:last_col])[3]
        slot_weight = jnp.einsum('bst,bt->bs', select[expert_id], weights[:, expert_id].astype(jnp.float32).reshape(blocks, TOK_DEV), precision=best_precision)
        update = update + jnp.einsum('bst,bsd->btd', select[expert_id], expert_out.reshape(blocks, CAP, D) * slot_weight[:, :, None], precision=best_precision)
    return (tokens_in.astype(jnp.float32) + update.reshape(TOKENS, D)).astype(jnp.bfloat16)


def backward_section(tokens_in, expert_ids, grad_out, router_table, gate_up, down_proj):
    select = slot_tables(expert_ids)
    onehot, gate_prob, weights = gating(tokens_in, expert_ids, router_table)
    blocks = select.shape[1]
    slot_back = jnp.zeros((blocks, TOK_DEV, D), jnp.float32)
    gate_grad = jnp.zeros(expert_ids.shape, jnp.float32)
    grads_gate, grads_up, grads_down = [], [], []
    for expert_id in range(FLIGHT):
        first_col = expert_id * FF
        last_col = first_col + FF
        w_gate = gate_up[0][:, first_col:last_col]
        w_up = gate_up[1][:, first_col:last_col]
        w_down = down_proj[first_col:last_col]
        gathered = pick_rows(select[expert_id], tokens_in).astype(jnp.bfloat16)
        grad_rows = pick_rows(select[expert_id], grad_out)
        slot_weight = jnp.einsum('bst,bt->bs', select[expert_id], weights[:, expert_id].astype(jnp.float32).reshape(blocks, TOK_DEV), precision=best_precision).reshape(-1)
        act_gate, act_up, hidden, expert_out = expert_parts(gathered, w_gate, w_up, w_down)
        scaled = (slot_weight[:, None] * grad_rows).astype(jnp.bfloat16)
        d_hidden = jnp.dot(scaled, w_down.T, preferred_element_type=jnp.float32)
        logistic = jax.nn.sigmoid(act_gate)
        d_gate = (d_hidden * act_up * logistic * (1.0 + act_gate * (1.0 - logistic))).astype(jnp.bfloat16)
        d_up = (d_hidden * act_gate * logistic).astype(jnp.bfloat16)
        row_count = gathered.shape[0]
        products = jnp.einsum('rwk,dwk->rwd', d_gate.astype(jnp.float32).reshape(row_count, WSPLIT, FF_DEV),
                              w_gate.astype(jnp.float32).reshape(D, WSPLIT, FF_DEV), precision=best_precision)
        products = products + jnp.einsum('rwk,dwk->rwd', d_up.astype(jnp.float32).reshape(row_count, WSPLIT, FF_DEV),
                                         w_up.astype(jnp.float32).reshape(D, WSPLIT, FF_DEV), precision=best_precision)
        slot_grad = shard_sum(products)
        gate_score = jnp.sum(grad_rows * expert_out, axis=1)
        slot_back = slot_back + jnp.einsum('bst,bsd->btd', select[expert_id], slot_grad.reshape(blocks, CAP, D), precision=best_precision)
        token_score = jnp.einsum('bst,bs->bt', select[expert_id], gate_score.reshape(blocks, CAP), precision=best_precision).reshape(TOKENS)
        gate_grad = gate_grad + token_score[:, None] * (expert_ids == expert_id).astype(jnp.float32)
        grads_gate.append(jnp.dot(gathered.T, d_gate, preferred_element_type=jnp.float32))
        grads_up.append(jnp.dot(gathered.T, d_up, preferred_element_type=jnp.float32))
        grads_down.append(jnp.dot(hidden.T, scaled, preferred_element_type=jnp.float32))
    logit_grad = gate_prob * (gate_grad - jnp.sum(gate_prob * gate_grad, axis=1, keepdims=True))
    logits_grad = jnp.sum(logit_grad[:, :, None] * onehot, axis=1).astype(jnp.bfloat16)
    router_back = jnp.dot(logits_grad, router_table.T, preferred_element_type=jnp.float32)
    back_grad = (grad_out.astype(jnp.float32) + slot_back.reshape(TOKENS, D) + router_back).astype(jnp.bfloat16)
    local_router = jnp.dot(tokens_in.T, logits_grad, preferred_element_type=jnp.float32).astype(jnp.bfloat16)
    local_gate_up = jnp.stack([jnp.concatenate(grads_gate, axis=1), jnp.concatenate(grads_up, axis=1)]).astype(jnp.bfloat16)
    local_down = jnp.concatenate(grads_down, axis=0).astype(jnp.bfloat16)
    return back_grad, local_gate_up, local_down, local_router


def twin_sum(stacked):
    return (stacked.astype(jnp.float32) + jnp.flip(stacked, 0).astype(jnp.float32)).astype(jnp.bfloat16)


def reference(section_in_a, route_a, router, gate_up, down_proj, section_in_b, route_b, grad_out_b):
    section_result = lax.map(lambda section_args: forward_section(*section_args), (section_in_a, route_a, router, gate_up, down_proj))
    back_grad, local_gate_up, local_down, local_router = lax.map(
        lambda section_args: backward_section(*section_args), (section_in_b, route_b, grad_out_b, router, gate_up, down_proj))
    return (jnp.roll(section_result, 1, axis=0), jnp.roll(back_grad, -1, axis=0),
            twin_sum(local_gate_up), twin_sum(local_down), twin_sum(local_router))
```

```python
import jax
import jax.numpy as jnp
from jax import lax
from jax.sharding import PartitionSpec as P

contract_last = (((1,), (1,)), ((), ()))
contract_first = (((0,), (0,)), ((), ()))


def ahead(count):
    return [(i, (i + 1) % count) for i in range(count)]


def behind(count):
    return [((i + 1) % count, i) for i in range(count)]


def twins(count):
    return [(i, count - 1 - i) for i in range(count)]


def across(count, bit):
    return [(i, i ^ bit) for i in range(count)]


def bits_of(count):
    return [1 << k for k in reversed(range(count.bit_length() - 1))]


def gathered_all(block, groups):
    me = lax.axis_index("expert")
    held = block[None]
    for bit in bits_of(groups):
        other = lax.ppermute(held, "expert", across(groups, bit))
        low = (me & bit) == 0
        held = jnp.stack([jnp.where(low, held, other), jnp.where(low, other, held)])
        held = held.reshape((-1,) + block.shape)
    steps = groups.bit_length() - 1
    held = held.reshape((2,) * steps + block.shape)
    held = held.transpose(tuple(reversed(range(steps))) + tuple(range(steps, held.ndim)))
    return held.reshape((groups,) + block.shape)


def scattered_sum(parts, groups):
    me = lax.axis_index("expert")
    steps = groups.bit_length() - 1
    rest = parts.shape[1:]
    held = parts.reshape((2,) * steps + rest)
    for step in range(steps):
        bit = 1 << step
        axis = steps - 1 - step
        first, second = (jnp.squeeze(h, axis) for h in jnp.split(held, 2, axis=axis))
        low = (me & bit) == 0
        other = lax.ppermute(jnp.where(low, second, first), "expert", across(groups, bit))
        total = jnp.where(low, first, second).astype(jnp.float32) + other.astype(jnp.float32)
        held = total if step == steps - 1 else total.astype(jnp.bfloat16)
    return held


def routing(expert_ids, flight, slot_count):
    tok_rows = expert_ids.shape[0]
    named_mask = jnp.stack(
        [jnp.any(expert_ids == expert_id, axis=1) for expert_id in range(flight)]
    ).astype(jnp.float32)
    earlier = (jnp.arange(tok_rows)[:, None] < jnp.arange(tok_rows)[None, :]).astype(jnp.bfloat16)
    order_rank = jnp.dot(
        named_mask.astype(jnp.bfloat16), earlier, preferred_element_type=jnp.float32
    )
    slot_ids = jnp.arange(slot_count, dtype=jnp.float32)
    chosen = named_mask[:, None, :] * (order_rank[:, None, :] == slot_ids[None, :, None])
    return chosen.astype(jnp.bfloat16).reshape(flight * slot_count, tok_rows)


def take(select, values):
    return jnp.dot(select, values, preferred_element_type=jnp.float32).astype(jnp.bfloat16)


def gating(rows, select, expert_ids, router_table, flight):
    experts = router_table.shape[1]
    slots = select.shape[0]
    ids = jnp.dot(select, expert_ids.astype(jnp.bfloat16), preferred_element_type=jnp.float32)
    filled = jnp.sum(select.astype(jnp.float32), axis=1)
    own = jnp.repeat(jnp.arange(flight, dtype=jnp.float32), slots // flight)
    logits = jnp.dot(rows, router_table, preferred_element_type=jnp.float32)
    lanes = jnp.arange(experts, dtype=jnp.float32)
    onehot = (ids[:, :, None] == lanes[None, None, :]).astype(jnp.float32)
    chosen = jnp.sum(onehot * logits[:, None, :], axis=2)
    gate_prob = jax.nn.softmax(chosen, axis=-1)
    named = (ids == own[:, None]).astype(jnp.float32) * filled[:, None]
    weight = jnp.sum(gate_prob * named, axis=1)
    slope = gate_prob * (named - weight[:, None])
    basis = jnp.sum(slope[:, :, None] * onehot, axis=1)
    return weight.astype(jnp.bfloat16), basis


def on_device(section_in_a, route_a, router, gate_up, down_proj, section_in_b, route_b, grad_out_b):
    groups = lax.axis_size("expert")
    pipe = lax.axis_size("pipe")
    me = lax.axis_index("expert")
    wsplit = min(8, groups)
    flight = groups // wsplit
    mine = me // wsplit
    tokens_a, tokens_b, grad_out = section_in_a[0], section_in_b[0], grad_out_b[0]
    tok_rows, model_width = tokens_a.shape
    slot_count = tok_rows // 8
    slots = flight * slot_count
    router_table = router[0]
    w_gate, w_up, w_down = gate_up[0, 0], gate_up[0, 1], down_proj[0]
    hidden_width = w_gate.shape[1]
    experts = router_table.shape[1]

    relayed_a = lax.ppermute(section_in_a, "pipe", ahead(pipe))[0]
    relayed_g = lax.ppermute(grad_out_b, "pipe", behind(pipe))[0]

    select_a = routing(route_a[0], flight, slot_count)
    select_b = routing(route_b[0], flight, slot_count)
    rows_a, rows_b, rows_g = (
        take(select_a, tokens_a),
        take(select_b, tokens_b),
        take(select_b, grad_out),
    )
    away_a = lax.ppermute(select_a, "pipe", ahead(pipe))
    away_b = lax.ppermute(select_b, "pipe", behind(pipe))

    packed = jnp.concatenate([rows_b, rows_g, rows_a])
    everywhere = gathered_all(packed, groups).reshape(groups, 3, flight, slot_count, model_width)
    twin_packed = lax.ppermute(packed[: 2 * slots], "pipe", twins(pipe))
    twin_rows = gathered_all(twin_packed, groups).reshape(
        groups, 2, flight, slot_count, model_width
    )

    weight_a, _ = gating(rows_a, select_a, route_a[0], router_table, flight)
    weight_b, basis = gating(rows_b, select_b, route_b[0], router_table, flight)
    small = gathered_all(
        jnp.concatenate([basis, weight_b.astype(jnp.float32)[:, None] * jnp.ones((1, experts))], 1),
        groups,
    )
    basis_all = small[:, :, :experts].reshape(groups * slots, experts)
    weight_all = small[:, :, experts].reshape(groups, flight, slot_count)

    def of_mine(values):
        return lax.dynamic_index_in_dim(values, mine, axis=1, keepdims=False)

    def flat(values):
        return of_mine(values).reshape(groups * slot_count, -1)

    def spread(values):
        values = values.reshape(groups, 1, slot_count, -1)
        here = (jnp.arange(flight) == mine)[None, :, None, None]
        return jnp.where(here, values, jnp.zeros((), values.dtype)).reshape(groups, slots, -1)

    def front(rows):
        act_gate = jnp.dot(rows, w_gate, preferred_element_type=jnp.float32)
        act_up = jnp.dot(rows, w_up, preferred_element_type=jnp.float32)
        return act_gate, act_up

    packed_rows, packed_grads = flat(everywhere[:, 0]), flat(everywhere[:, 1])
    weights = of_mine(weight_all).reshape(-1, 1)
    act_gate, act_up = front(packed_rows)
    back = lax.dot_general(packed_grads, w_down, contract_last, preferred_element_type=jnp.float32)
    logistic = jax.nn.sigmoid(act_gate)
    hidden = act_gate * logistic * act_up
    score_part = jnp.sum(hidden * back, axis=1)
    scores = jnp.sum(gathered_all(spread(score_part[:, None])[:, :, 0], groups), axis=0)
    logits_grad = (scores.reshape(-1, 1) * basis_all).astype(jnp.bfloat16)
    d_hidden = weights * back
    d_gate = (d_hidden * act_up * logistic * (1.0 + act_gate * (1.0 - logistic))).astype(
        jnp.bfloat16
    )
    d_up = (d_hidden * act_gate * logistic).astype(jnp.bfloat16)
    weighed = (hidden * weights).astype(jnp.bfloat16)
    slot_part = (
        lax.dot_general(d_gate, w_gate, contract_last, preferred_element_type=jnp.float32)
        + lax.dot_general(d_up, w_up, contract_last, preferred_element_type=jnp.float32)
    ).astype(jnp.bfloat16)
    slot_back = scattered_sum(spread(slot_part), groups)
    my_logits_grad = lax.dynamic_index_in_dim(
        logits_grad.reshape(groups, slots, experts), me, axis=0, keepdims=False
    )
    router_back = lax.dot_general(
        my_logits_grad, router_table, contract_last, preferred_element_type=jnp.float32
    )
    sent_b = lax.ppermute(
        (slot_back + router_back).astype(jnp.bfloat16), "pipe", behind(pipe)
    )
    grad_in_b = (
        relayed_g.astype(jnp.float32)
        + lax.dot_general(away_b, sent_b, contract_first, preferred_element_type=jnp.float32)
    ).astype(jnp.bfloat16)

    gate_a, up_a = front(flat(everywhere[:, 2]))
    hidden_a = (jax.nn.silu(gate_a) * up_a).astype(jnp.bfloat16)
    part_a = jnp.dot(hidden_a, w_down, preferred_element_type=jnp.float32).astype(jnp.bfloat16)
    out_a = scattered_sum(spread(part_a), groups)
    sent_a = lax.ppermute(
        (out_a * weight_a.astype(jnp.float32)[:, None]).astype(jnp.bfloat16), "pipe", ahead(pipe)
    )
    section_out_a = (
        relayed_a.astype(jnp.float32)
        + lax.dot_general(away_a, sent_a, contract_first, preferred_element_type=jnp.float32)
    ).astype(jnp.bfloat16)

    factors = jnp.concatenate([d_gate, d_up, weighed], axis=1)
    twin_factors = lax.ppermute(factors, "pipe", twins(pipe))
    twin_logits_grad = lax.ppermute(logits_grad, "pipe", twins(pipe))
    both_rows = jnp.concatenate([packed_rows, flat(twin_rows[:, 0])])
    both_grads = jnp.concatenate([packed_grads, flat(twin_rows[:, 1])])
    both_factors = jnp.concatenate([factors, twin_factors])
    grad_gate_up = jnp.stack(
        [
            lax.dot_general(
                both_rows,
                both_factors[:, k * hidden_width : (k + 1) * hidden_width],
                contract_first,
                preferred_element_type=jnp.float32,
            ).astype(jnp.bfloat16)
            for k in range(2)
        ]
    )
    grad_down = lax.dot_general(
        both_factors[:, 2 * hidden_width :],
        both_grads,
        contract_first,
        preferred_element_type=jnp.float32,
    ).astype(jnp.bfloat16)
    share = model_width // groups
    all_rows = jnp.concatenate([everywhere[:, 0], twin_rows[:, 0]]).reshape(-1, model_width)
    grad_router = lax.dot_general(
        lax.dynamic_slice_in_dim(all_rows, me * share, share, axis=1),
        jnp.concatenate([logits_grad, twin_logits_grad]),
        contract_first,
        preferred_element_type=jnp.float32,
    ).astype(jnp.bfloat16)
    return (
        section_out_a[None],
        grad_in_b[None],
        grad_gate_up[None],
        grad_down[None],
        grad_router[None],
    )


def solution(mesh):
    return jax.shard_map(
        on_device,
        mesh=mesh,
        in_specs=(
            P("pipe", "expert", None),
            P("pipe", "expert", None),
            P("pipe", None, None),
            P("pipe", None, None, "expert"),
            P("pipe", "expert", None),
            P("pipe", "expert", None),
            P("pipe", "expert", None),
            P("pipe", "expert", None),
        ),
        out_specs=(
            P("pipe", "expert", None),
            P("pipe", "expert", None),
            P("pipe", None, None, "expert"),
            P("pipe", "expert", None),
            P("pipe", "expert", None),
        ),
        check_vma=False,
    )
```

```python
import functools

import jax
import jax.numpy as jnp
from jax import lax
from jax.experimental import pallas as pl
from jax.experimental.pallas import tpu as pltpu
from jax.sharding import PartitionSpec as P

F32, BF16 = jnp.float32, jnp.bfloat16
whole = pl.BlockSpec(memory_space=pltpu.VMEM)
scalar = pl.BlockSpec(memory_space=pltpu.SMEM)
last_last = (((1,), (1,)), ((), ()))
first_first = (((0,), (0,)), ((), ()))
MIB = 1 << 20


def dot(a, b, dims=(((1,), (0,)), ((), ()))):
    return lax.dot_general(a, b, dims, preferred_element_type=F32)


def ahead(count):
    return [(i, (i + 1) % count) for i in range(count)]


def behind(count):
    return [((i + 1) % count, i) for i in range(count)]


def twins(count):
    return [(i, count - 1 - i) for i in range(count)]


def exchanged(block, bit):
    count = lax.axis_size("expert")
    return lax.ppermute(block, "expert", [(i, i ^ bit) for i in range(count)])


def call(kernel, outs, args, limit=32, cost=None, **more):
    return pl.pallas_call(
        kernel,
        out_shape=[jax.ShapeDtypeStruct(shape, dtype) for shape, dtype in outs],
        compiler_params=pltpu.CompilerParams(vmem_limit_bytes=limit * MIB),
        cost_estimate=pl.CostEstimate(flops=cost[0], bytes_accessed=cost[1], transcendentals=0),
        **more,
    )(*args)


def slot_select(ids, flight, slot_count):
    tokens = ids.shape[1]
    earlier = (
        lax.broadcasted_iota(jnp.int32, (tokens, tokens), 0)
        < lax.broadcasted_iota(jnp.int32, (tokens, tokens), 1)
    ).astype(F32).astype(BF16)
    slot_ids = lax.broadcasted_iota(jnp.int32, (slot_count, tokens), 0).astype(F32)
    picked = []
    for f in range(flight):
        named = jnp.max((ids == f).astype(F32), axis=0, keepdims=True)
        named = jnp.broadcast_to(named, (slot_count, tokens))
        rank = dot(named.astype(BF16), earlier)
        picked.append(jnp.where(rank == slot_ids, named, 0.0))
    return jnp.concatenate(picked, axis=0).astype(BF16)


def pick_kernel(flight, slot_count, ids_a, ids_b, x_a, x_b, grad, packed, twin, sel_a, sel_b):
    width = x_a.shape[1]
    tokens = x_a.shape[0]
    for ids_ref, select_ref, sources in ((ids_b, sel_b, ((0, x_b), (1, grad))), (ids_a, sel_a, ((2, x_a),))):
        ids = ids_ref[...]
        select = slot_select(ids, flight, slot_count)
        select_ref[...] = select
        spare = jnp.zeros((packed.shape[2] - width - ids.shape[0], tokens), F32)
        lanes = jnp.concatenate([ids.astype(F32), spare], axis=0).astype(BF16)
        slot_ids = dot(select, lanes, last_last).astype(BF16)
        for place, source in sources:
            rows = dot(select, source[...]).astype(BF16)
            packed[place, :, :width] = rows
            packed[place, :, width:] = slot_ids
            if place < 2:
                twin[place] = rows


def gates(ids, logits, topk, expert):
    lanes = lax.broadcasted_iota(jnp.int32, logits.shape, 1).astype(F32)
    picks = [ids[:, k : k + 1] for k in range(topk)]
    chosen = [
        jnp.sum(jnp.where(lanes == pick, logits, 0.0), axis=1, keepdims=True) for pick in picks
    ]
    top = functools.reduce(jnp.maximum, chosen)
    powers = [jnp.exp(value - top) for value in chosen]
    scale = 1.0 / functools.reduce(jnp.add, powers)
    probs = [power * scale for power in powers]
    named = [(pick == expert).astype(F32) for pick in picks]
    weight = functools.reduce(jnp.add, [p * n for p, n in zip(probs, named)])
    basis = functools.reduce(
        jnp.add,
        [jnp.where(lanes == pick, p * (n - weight), 0.0) for pick, p, n in zip(picks, probs, named)],
    )
    return weight, basis


def expert_kernel(counts, topk, mine, *refs):
    pieces, refs = refs[: len(counts)], refs[len(counts) :]
    router, gate_up, down, keep, send, lg_part, factors, rows, grads, ids = refs
    slot_count = pieces[0].shape[2]
    width, hidden_width = gate_up.shape[1], gate_up.shape[2]
    blocks = sum(counts)
    half = blocks * slot_count
    place = 0
    for piece, count in zip(pieces, counts):
        for j in range(count):
            here = pl.ds(place * slot_count, slot_count)
            there = pl.ds(half + place * slot_count, slot_count)
            rows[here, :] = piece[j, 0, :, :width]
            rows[there, :] = piece[j, 2, :, :width]
            grads[here, :] = piece[j, 1, :, :width]
            ids[here, :] = piece[j, 0, :, width:].astype(F32)
            ids[there, :] = piece[j, 2, :, width:].astype(F32)
            place += 1
    expert = mine[0].astype(F32)
    logits = dot(rows[...], router[...])
    act_gate = dot(rows[...], gate_up[0])
    act_up = dot(rows[...], gate_up[1])
    back = dot(grads[...], down[...], last_last)
    weight, basis = gates(ids[...], logits, topk, expert)
    logistic = jax.nn.sigmoid(act_gate)
    hidden = act_gate * logistic * act_up
    weight_b = weight[:half]
    hidden_b, gate_b, up_b, log_b = hidden[:half], act_gate[:half], act_up[:half], logistic[:half]
    lg_part[...] = (
        jnp.sum(hidden_b * back, axis=1, keepdims=True) * basis[:half]
    ).reshape(lg_part.shape)
    d_hidden = weight_b * back
    d_gate = (d_hidden * up_b * log_b * (1.0 + gate_b * (1.0 - log_b))).astype(BF16)
    d_up = (d_hidden * gate_b * log_b).astype(BF16)
    factors[:, :hidden_width] = d_gate
    factors[:, hidden_width : 2 * hidden_width] = d_up
    factors[:, 2 * hidden_width :] = (weight_b * hidden_b).astype(BF16)
    hidden_a = (weight[half:] * hidden[half:]).astype(BF16)
    step = min(width, 512)
    for first in range(0, width, step):
        cols = slice(first, first + step)
        part_a = dot(hidden_a, down[:, cols]).astype(BF16)
        part_b = (
            dot(d_gate, gate_up[0, cols, :], last_last) + dot(d_up, gate_up[1, cols, :], last_last)
        ).astype(BF16)
        for j in range(blocks):
            out, k = (keep, j) if j < blocks // 2 else (send, j - blocks // 2)
            here = slice(j * slot_count, (j + 1) * slot_count)
            out[k, :, cols] = part_a[here]
            out[k, :, first + width : first + width + step] = part_b[here]


def flipped_sum(lg, lg_in, blocks, span):
    return [lg[j] + lg_in[j ^ span] for j in range(blocks)]


def middle_kernel(span, keep, recv, lg, lg_in, keep_out, send_out, lg_out):
    count = keep.shape[0] // 2
    for j in range(keep.shape[0]):
        total = (keep[j].astype(F32) + recv[j].astype(F32)).astype(BF16)
        if j < count:
            keep_out[j] = total
        else:
            send_out[j - count] = total
    for j, value in enumerate(flipped_sum(lg, lg_in, lg.shape[0], span)):
        lg_out[j] = value


def last_kernel(span, keep, recv, lg, lg_in, router, factors, sel_a, sel_b, out_a, out_b, wide):
    width = router.shape[0]
    total = keep[0].astype(F32) + recv[0].astype(F32)
    sums = [value.astype(BF16) for value in flipped_sum(lg, lg_in, lg.shape[0], span)]
    out_a[:, :width] = total[:, :width].astype(BF16)
    out_a[:, width:] = sel_a[...]
    out_b[:, :width] = (total[:, width:] + dot(sums[0], router[...], last_last)).astype(BF16)
    out_b[:, width:] = sel_b[...]
    slot_count = factors.shape[0] // lg.shape[0]
    core = factors.shape[1]
    experts = router.shape[1]
    for j, value in enumerate(sums):
        wide[j, :, :core] = factors[j * slot_count : (j + 1) * slot_count, :]
        for f in range(value.shape[0] // slot_count):
            wide[j, :, core + f * experts : core + (f + 1) * experts] = value[
                f * slot_count : (f + 1) * slot_count
            ]


def grads_kernel(own_counts, width, hidden_width, experts, same, me, *refs):
    count = len(own_counts)
    own, twin, refs = refs[:count], refs[count : 2 * count], refs[2 * count :]
    own_all, twin_all = own, twin
    if not same:
        own_all, twin_all, refs = refs[:count], refs[count : 2 * count], refs[2 * count :]
    own_wide, twin_wide, gate_up, down, router = refs
    i = pl.program_id(0)
    tile, share_tile = down.shape[1], router.shape[0]
    share = share_tile * pl.num_programs(0)
    cols = pl.ds(pl.multiple_of(i * tile, tile), tile)
    mine = pl.ds(pl.multiple_of(me[0] * share + i * share_tile, 128), share_tile)

    def stacked(groups, which, where):
        return jnp.concatenate(
            [p[j, which, :, where] for pieces in groups for p, n in zip(pieces, own_counts) for j in range(n)]
        )

    def column(first, size):
        return jnp.concatenate(
            [w[j, :, first : first + size] for w in (own_wide, twin_wide) for j in range(w.shape[0])]
        )

    core = 3 * hidden_width
    rows = stacked((own, twin), 0, cols)
    both = dot(rows, column(0, 2 * hidden_width), first_first).astype(BF16)
    gate_up[0] = both[:, :hidden_width]
    gate_up[1] = both[:, hidden_width:]
    down[...] = dot(
        column(2 * hidden_width, hidden_width), stacked((own, twin), 1, cols), first_first
    ).astype(BF16)
    flight = (own_wide.shape[2] - core) // experts
    lg = jnp.concatenate(
        [
            w[j, :, core + f * experts : core + (f + 1) * experts]
            for w in (own_wide, twin_wide)
            for j in range(w.shape[0])
            for f in range(flight)
        ]
    )
    router[...] = dot(stacked((own_all, twin_all), 0, mine), lg, first_first).astype(BF16)


def place_kernel(base, sent, select, out):
    out[...] = (base[...].astype(F32) + dot(select[...], sent[...], first_first)).astype(BF16)


def placed(base, sent):
    tokens, width = base.shape
    slots = sent.shape[0]
    tile = width // 4
    return call(
        place_kernel,
        [((tokens, width), BF16)],
        (base, sent, sent),
        cost=(2 * tokens * slots * width, 4 * tokens * width),
        grid=(width // tile,),
        in_specs=[
            pl.BlockSpec((tokens, tile), lambda i: (0, i)),
            pl.BlockSpec((slots, tile), lambda i: (0, i)),
            pl.BlockSpec((slots, tokens), lambda i: (0, width // tokens)),
        ],
        out_specs=[pl.BlockSpec((tokens, tile), lambda i: (0, i))],
    )[0]


def on_device(section_in_a, route_a, router, gate_up, down_proj, section_in_b, route_b, grad_out_b):
    groups = lax.axis_size("expert")
    pipe = lax.axis_size("pipe")
    me = lax.axis_index("expert")
    wsplit = min(8, groups)
    flight = groups // wsplit
    mine = me // wsplit
    tok_rows, width = section_in_a.shape[1:]
    topk = route_a.shape[2]
    slot_count = tok_rows // 8
    slots = flight * slot_count
    router_table = router[0]
    experts = router_table.shape[1]
    hidden_width = gate_up.shape[3]
    bits = [1 << k for k in reversed(range(groups.bit_length() - 1))]

    relayed_a = lax.ppermute(section_in_a, "pipe", ahead(pipe))[0]
    packed, twin_rows, sel_a, sel_b = call(
        functools.partial(pick_kernel, flight, slot_count),
        [
            ((3, slots, width + experts), BF16),
            ((2, slots, width), BF16),
            ((slots, tok_rows), BF16),
            ((slots, tok_rows), BF16),
        ],
        (route_a[0].T, route_b[0].T, section_in_a[0], section_in_b[0], grad_out_b[0]),
        cost=(6 * slots * tok_rows * width, 8 * tok_rows * width),
        in_specs=[whole] * 5,
        out_specs=[whole] * 4,
    )

    def everywhere(block):
        pieces = [block[None]]
        for bit in bits:
            held = pieces[0] if len(pieces) == 1 else jnp.concatenate(pieces)
            pieces.append(exchanged(held, bit))
        return pieces

    def of_mine(piece):
        if flight == 1:
            return piece
        split = piece.reshape(piece.shape[:2] + (flight, slot_count) + piece.shape[3:])
        return lax.dynamic_index_in_dim(split, mine, axis=2, keepdims=False)

    def spread(values):
        if flight == 1:
            return values
        here = (jnp.arange(flight) == mine)[None, :, None, None]
        full = jnp.where(here, values[:, None], jnp.zeros((), values.dtype))
        return full.reshape(values.shape[0], slots, values.shape[2])

    own_all = everywhere(packed)
    relayed_g = lax.ppermute(grad_out_b, "pipe", behind(pipe))[0]
    twin_all = everywhere(lax.ppermute(twin_rows, "pipe", twins(pipe)))
    own = [of_mine(p) for p in own_all]
    twin = [of_mine(p) for p in twin_all]
    counts = [p.shape[0] for p in own]
    rows_all = groups * slot_count

    keep, send, lg, factors = call(
        functools.partial(expert_kernel, counts, topk),
        [
            ((groups // 2, slot_count, 2 * width), BF16),
            ((groups // 2, slot_count, 2 * width), BF16),
            ((groups, slot_count, experts), F32),
            ((rows_all, 3 * hidden_width), BF16),
        ],
        (mine.reshape(1), *own, router_table, gate_up[0], down_proj[0]),
        cost=(20 * rows_all * width * hidden_width, 6 * width * hidden_width),
        in_specs=[scalar] + [whole] * (len(own) + 3),
        out_specs=[whole] * 4,
        scratch_shapes=[
            pltpu.VMEM((2 * rows_all, width), BF16),
            pltpu.VMEM((rows_all, width), BF16),
            pltpu.VMEM((2 * rows_all, experts), F32),
        ],
    )
    keep, send, lg = spread(keep), spread(send), spread(lg)
    for step, bit in enumerate(reversed(bits)):
        recv, lg_in = exchanged(send, bit), exchanged(lg, bit)
        span = groups >> (step + 1)
        if step < len(bits) - 1:
            half = (keep.shape[0] // 2,) + keep.shape[1:]
            keep, send, lg = call(
                functools.partial(middle_kernel, span),
                [(half, BF16), (half, BF16), (lg.shape, F32)],
                (keep, recv, lg, lg_in),
                cost=(keep.size, 6 * keep.size),
                in_specs=[whole] * 4,
                out_specs=[whole] * 3,
            )
    sent_a, sent_b, wide = call(
        functools.partial(last_kernel, span),
        [
            ((slots, width + tok_rows), BF16),
            ((slots, width + tok_rows), BF16),
            ((groups, slot_count, 3 * hidden_width + flight * experts), BF16),
        ],
        (keep, recv, lg, lg_in, router_table, factors, sel_a, sel_b),
        cost=(2 * slots * width * experts, 2 * width * experts),
        in_specs=[whole] * 8,
        out_specs=[whole] * 3,
    )
    last_b = lax.ppermute(sent_b, "pipe", behind(pipe))
    twin_wide = lax.ppermute(wide, "pipe", twins(pipe))
    last_a = lax.ppermute(sent_a, "pipe", ahead(pipe))

    share = width // groups
    tiles = min(8, share // 128)
    tile = width // tiles
    same = flight == 1
    held = (*own, *twin) if same else (*own, *twin, *own_all, *twin_all)
    grad_gate_up, grad_down, grad_router = call(
        functools.partial(grads_kernel, counts, width, hidden_width, experts, same),
        [
            ((2, width, hidden_width), BF16),
            ((hidden_width, width), BF16),
            ((share, experts), BF16),
        ],
        (me.reshape(1), *held, wide, twin_wide),
        cost=(12 * rows_all * width * hidden_width, 6 * width * hidden_width),
        grid=(tiles,),
        in_specs=[scalar] + [whole] * (len(held) + 2),
        out_specs=[
            pl.BlockSpec((2, tile, hidden_width), lambda i: (0, i, 0)),
            pl.BlockSpec((hidden_width, tile), lambda i: (0, i)),
            pl.BlockSpec((share // tiles, experts), lambda i: (i, 0)),
        ],
    )
    grad_in_b = placed(relayed_g, last_b)
    section_out_a = placed(relayed_a, last_a)
    return (
        section_out_a[None],
        grad_in_b[None],
        grad_gate_up[None],
        grad_down[None],
        grad_router[None],
    )


def solution(mesh):
    return jax.shard_map(
        on_device,
        mesh=mesh,
        in_specs=(
            P("pipe", "expert", None),
            P("pipe", "expert", None),
            P("pipe", None, None),
            P("pipe", None, None, "expert"),
            P("pipe", "expert", None),
            P("pipe", "expert", None),
            P("pipe", "expert", None),
            P("pipe", "expert", None),
        ),
        out_specs=(
            P("pipe", "expert", None),
            P("pipe", "expert", None),
            P("pipe", None, None, "expert"),
            P("pipe", "expert", None),
            P("pipe", "expert", None),
        ),
        check_vma=False,
    )
```

```python
import functools

import jax
import jax.numpy as jnp
from jax import lax
from jax.experimental import pallas as pl
from jax.experimental.pallas import tpu as pltpu
from jax.sharding import PartitionSpec as P

F32, BF16 = jnp.float32, jnp.bfloat16
whole = pl.BlockSpec(memory_space=pltpu.VMEM)
anywhere = pl.BlockSpec(memory_space=pl.ANY)
outside = pl.BlockSpec(memory_space=pltpu.HBM)
scalar = pl.BlockSpec(memory_space=pltpu.SMEM)
last_last = (((1,), (1,)), ((), ()))
first_first = (((0,), (0,)), ((), ()))
MIB = 1 << 20


def dot(a, b, dims=(((1,), (0,)), ((), ()))):
    return lax.dot_general(a, b, dims, preferred_element_type=F32)


def near(count):
    return [(i, i ^ 1) for i in range(count)]


def far(count):
    return [(i, (i + 1 if i % 2 else i - 1) % count) for i in range(count)]


def twins(count):
    return [(i, count - 1 - i) for i in range(count)]


def exchanged(block, bit):
    count = lax.axis_size("expert")
    return lax.ppermute(block, "expert", [(i, i ^ bit) for i in range(count)])


def call(kernel, outs, args, limit=24, **more):
    return pl.pallas_call(
        kernel,
        out_shape=[jax.ShapeDtypeStruct(shape, dtype) for shape, dtype in outs],
        compiler_params=pltpu.CompilerParams(vmem_limit_bytes=limit * MIB),
        cost_estimate=pl.CostEstimate(flops=0, bytes_accessed=0, transcendentals=0),
        **more,
    )(*args)


def slot_select(ids, flight, slot_count):
    tokens = ids.shape[1]
    earlier = (
        lax.broadcasted_iota(jnp.int32, (tokens, tokens), 0)
        < lax.broadcasted_iota(jnp.int32, (tokens, tokens), 1)
    ).astype(F32).astype(BF16)
    slot_ids = lax.broadcasted_iota(jnp.int32, (slot_count, tokens), 0).astype(F32)
    picked = []
    for f in range(flight):
        named = jnp.max((ids == f).astype(F32), axis=0, keepdims=True)
        named = jnp.broadcast_to(named, (slot_count, tokens))
        rank = dot(named.astype(BF16), earlier)
        picked.append(jnp.where(rank == slot_ids, named, 0.0))
    return jnp.concatenate(picked, axis=0).astype(BF16)


def pick_kernel(flight, slot_count, topk, odd, *refs):
    sources, refs = refs[:5], refs[5:]
    packed, twin, sel_a, sel_b, to_near = refs[:5]
    held, sems = refs[5:10], refs[10]
    copies = [
        pltpu.make_async_copy(source, here, sems.at[k])
        for k, (source, here) in enumerate(zip(sources, held))
    ]
    for copy in copies:
        copy.start()
    ids_b, ids_a, x_b, grad, x_a = held
    tokens, width = x_b.shape
    lanes = packed.shape[2] - width
    for k, (ids_ref, select_ref) in enumerate(((ids_b, sel_b), (ids_a, sel_a))):
        copies[k].wait()
        ids = ids_ref[...]
        select = slot_select(ids, flight, slot_count)
        select_ref[...] = select
        spare = jnp.zeros((lanes - topk, tokens), F32)
        numbers = jnp.concatenate([ids.astype(F32), spare], axis=0).astype(BF16)
        slot_ids = dot(select, numbers, last_last).astype(BF16)
        for place, source in ((0, 2), (1, 3)) if k == 0 else ((2, 4),):
            copies[source].wait()
            if place > 0:
                @pl.when(odd[0] == (1 if place == 1 else 0))
                def _(onward=held[source]):
                    pltpu.make_async_copy(onward, to_near.at[0], sems.at[5]).start()

            rows = dot(select, held[source][...]).astype(BF16)
            packed[place, :, :width] = rows
            packed[place, :, width:] = slot_ids
            if place < 2:
                twin[place] = rows
    pltpu.make_async_copy(x_a, to_near.at[0], sems.at[5]).wait()


def order_kernel(flight, slots, odd, ids_a, ids_b, x_a, grad, first, at, far, ids, block, sems):
    for mine, ids_ref, block_ref in ((1, ids_a, x_a), (0, ids_b, grad)):

        @pl.when(odd[0] == mine)
        def _(ids_ref=ids_ref, block_ref=block_ref):
            pltpu.make_async_copy(ids_ref, ids, sems.at[0]).start()
            pltpu.make_async_copy(block_ref, block, sems.at[1]).start()

    tokens = block.shape[0]
    earlier = (
        lax.broadcasted_iota(jnp.int32, (tokens, tokens), 0)
        < lax.broadcasted_iota(jnp.int32, (tokens, tokens), 1)
    ).astype(F32).astype(BF16)
    place = lax.broadcasted_iota(jnp.int32, (tokens, tokens), 0).astype(F32)
    token = lax.broadcasted_iota(jnp.int32, (8, tokens), 1).astype(F32)
    pltpu.make_async_copy(ids_a, ids, sems.at[0]).wait()
    named = jnp.max((ids[...] < flight).astype(F32), axis=0, keepdims=True)
    named = jnp.broadcast_to(named, (8, tokens))
    rank = dot(named.astype(BF16), earlier)
    count = jnp.sum(named, axis=1, keepdims=True)
    where = jnp.where(named > 0.0, rank, count + token - rank)[:1]
    at[...] = jnp.broadcast_to(where, at.shape).astype(BF16)
    order = (place == where).astype(F32).astype(BF16)
    pltpu.make_async_copy(x_a, block, sems.at[1]).wait()
    rows = dot(order, block[...]).astype(BF16)
    first[...] = rows[:slots, :]
    far[...] = rows[slots:, :]


def gates(ids, logits, topk, expert):
    lanes = lax.broadcasted_iota(jnp.int32, logits.shape, 1).astype(F32)
    picks = [ids[:, k : k + 1] for k in range(topk)]
    chosen = [
        jnp.sum(jnp.where(lanes == pick, logits, 0.0), axis=1, keepdims=True) for pick in picks
    ]
    top = functools.reduce(jnp.maximum, chosen)
    powers = [jnp.exp(value - top) for value in chosen]
    scale = 1.0 / functools.reduce(jnp.add, powers)
    probs = [power * scale for power in powers]
    named = [(pick == expert).astype(F32) for pick in picks]
    weight = functools.reduce(jnp.add, [p * n for p, n in zip(probs, named)])
    basis = functools.reduce(
        jnp.add,
        [jnp.where(lanes == pick, p * (n - weight), 0.0) for pick, p, n in zip(picks, probs, named)],
    )
    return weight, basis


def coded(columns, lanes):
    rows = columns[0].shape[0]
    lane = lax.broadcasted_iota(jnp.int32, (rows, lanes), 1)
    out = jnp.zeros((rows, lanes), F32)
    for j, rest in enumerate(columns):
        for k in range(3):
            term = rest.astype(BF16).astype(F32)
            out = jnp.where(lane == 3 * j + k, term, out)
            rest = rest - term
    return out.astype(BF16)


def decoded(code, count):
    code = code.astype(F32)
    return [
        code[:, 3 * j : 3 * j + 1] + code[:, 3 * j + 1 : 3 * j + 2] + code[:, 3 * j + 2 : 3 * j + 3]
        for j in range(count)
    ]


def summed_scores(own, other, blocks, span, width):
    mine, theirs = decoded(own[:, width:], blocks), decoded(other[:, width:], blocks)
    return [mine[j] + theirs[j ^ span] for j in range(blocks)]


def expert_kernel(blocks, topk, mine, *refs):
    pieces, refs = refs[:blocks], refs[blocks:]
    (router, gate_up, down), refs = refs[:3], refs[3:]
    parts, refs = refs[:blocks], refs[blocks:]
    basis_out, factors, rows, grads, ids = refs
    slot_count = pieces[0].shape[1]
    width, hidden_width = gate_up.shape[1], gate_up.shape[2]
    half = blocks * slot_count
    for place in range(blocks):
        piece = pieces[place]
        here = pl.ds(place * slot_count, slot_count)
        there = pl.ds(half + place * slot_count, slot_count)
        rows[here, :] = piece[0, :, :width]
        rows[there, :] = piece[2, :, :width]
        grads[here, :] = piece[1, :, :width]
        ids[here, :] = piece[0, :, width:].astype(F32)
        ids[there, :] = piece[2, :, width:].astype(F32)
    weight, basis = gates(ids[...], dot(rows[...], router[...]), topk, mine[0].astype(F32))
    act_gate = dot(rows[...], gate_up[0])
    act_up = dot(rows[...], gate_up[1])
    back = dot(grads[...], down[...], last_last)
    logistic = jax.nn.sigmoid(act_gate)
    hidden = act_gate * logistic * act_up
    weight_b = weight[:half]
    hidden_b, gate_b, up_b, log_b = hidden[:half], act_gate[:half], act_up[:half], logistic[:half]
    basis_out[...] = basis[:half].reshape(basis_out.shape)
    scores = jnp.sum(hidden_b * back, axis=1, keepdims=True)
    code = coded(
        [scores[j * slot_count : (j + 1) * slot_count] for j in range(blocks)],
        parts[0].shape[1] - 2 * width,
    )
    d_hidden = weight_b * back
    d_gate = (d_hidden * up_b * log_b * (1.0 + gate_b * (1.0 - log_b))).astype(BF16)
    d_up = (d_hidden * gate_b * log_b).astype(BF16)
    factors[:, :hidden_width] = d_gate
    factors[:, hidden_width : 2 * hidden_width] = d_up
    factors[:, 2 * hidden_width :] = (weight_b * hidden_b).astype(BF16)
    hidden_a = (weight[half:] * hidden[half:]).astype(BF16)
    step = min(width, 512)
    for first in range(0, width, step):
        cols = slice(first, first + step)
        part_a = dot(hidden_a, down[:, cols]).astype(BF16)
        part_b = (
            dot(d_gate, gate_up[0, cols, :], last_last) + dot(d_up, gate_up[1, cols, :], last_last)
        ).astype(BF16)
        for j, part in enumerate(parts):
            here = slice(j * slot_count, (j + 1) * slot_count)
            part[:, cols] = part_a[here]
            part[:, first + width : first + width + step] = part_b[here]
    for part in parts:
        part[:, 2 * width :] = code


def added(terms, width):
    return functools.reduce(jnp.add, [term[:, :width].astype(F32) for term in terms])


def middle_kernel(blocks, span, sizes, split, own, other, *refs):
    terms, outs = refs[: sum(sizes)], refs[sum(sizes) + blocks :]
    lanes = own.shape[1] - 128
    code = coded(summed_scores(own, other, blocks, span, lanes), 128)
    for size in sizes:
        total = added(terms[:size], lanes).astype(BF16)
        if split:
            outs[0][...] = total[:, : lanes // 2]
            outs[1][:, : lanes // 2] = total[:, lanes // 2 :]
            outs[1][:, lanes // 2 :] = code
        else:
            outs[0][:, :lanes] = total
            outs[0][:, lanes:] = code
            outs = outs[1:]
        terms = terms[size:]


def last_kernel(blocks, span, count, odd, own, *refs):
    terms, refs = refs[: count - 2], refs[count - 2 :]
    last_a, last_b, basis, router, factors, sel_a, sel_b, first, at, to_near, to_far, wide = refs
    width, experts = router.shape
    slots = first.shape[0]
    total = added(terms, 2 * width)
    scores = summed_scores(own, last_b, blocks, span, width)
    sums = [(score * basis[j]).astype(BF16) for j, score in enumerate(scores)]
    more_a = total[:, :width] + last_a[...].astype(F32)
    more_b = (
        total[:, width:] + last_b[:, :width].astype(F32) + dot(sums[0], router[...], last_last)
    )
    even = odd[0] == 0
    to_near[:, :width] = jnp.where(even, more_a, more_b).astype(BF16)
    to_near[:, width:] = jnp.where(even, sel_a[...], sel_b[...])
    more = jnp.where(even, more_b, more_a)
    if slots * blocks != factors.shape[0]:
        place = lax.broadcasted_iota(jnp.int32, at.shape, 0).astype(F32)
        row = (place == at[...].astype(F32)).astype(F32).astype(BF16)
        slot = jnp.where(even, sel_b[...].astype(F32), sel_a[...].astype(F32)).astype(BF16)
        more = jnp.dot(dot(row, slot, last_last), more, precision=lax.Precision.HIGHEST)
    to_far[:, :width] = (first[...].astype(F32) + more).astype(BF16)
    to_far[:, width:] = at[...]
    slot_count = factors.shape[0] // blocks
    core = factors.shape[1]
    for j, value in enumerate(sums):
        wide[j, :, :core] = factors[j * slot_count : (j + 1) * slot_count, :]
        for f in range(value.shape[0] // slot_count):
            wide[j, :, core + f * experts : core + (f + 1) * experts] = value[
                f * slot_count : (f + 1) * slot_count
            ]


def grads_kernel(blocks, hidden_width, experts, same, me, *refs):
    pieces, refs = refs[: 2 * blocks], refs[2 * blocks :]
    pieces_all = pieces
    if not same:
        pieces_all, refs = refs[: 2 * blocks], refs[2 * blocks :]
    own_wide, twin_wide, gate_up, down, router = refs
    i = pl.program_id(0)
    tile, share_tile = down.shape[1], router.shape[0]
    share = share_tile * pl.num_programs(0)
    cols = pl.ds(pl.multiple_of(i * tile, tile), tile)
    mine = pl.ds(pl.multiple_of(me[0] * share + i * share_tile, 128), share_tile)

    def stacked(held, which, where):
        return jnp.concatenate([piece[which, :, where] for piece in held])

    def column(first, size):
        return jnp.concatenate(
            [w[j, :, first : first + size] for w in (own_wide, twin_wide) for j in range(blocks)]
        )

    core = 3 * hidden_width
    both = dot(stacked(pieces, 0, cols), column(0, 2 * hidden_width), first_first).astype(BF16)
    gate_up[0] = both[:, :hidden_width]
    gate_up[1] = both[:, hidden_width:]
    down[...] = dot(
        column(2 * hidden_width, hidden_width), stacked(pieces, 1, cols), first_first
    ).astype(BF16)
    flight = (own_wide.shape[2] - core) // experts
    lg = jnp.concatenate(
        [
            w[j, :, core + f * experts : core + (f + 1) * experts]
            for w in (own_wide, twin_wide)
            for j in range(blocks)
            for f in range(flight)
        ]
    )
    router[...] = dot(stacked(pieces_all, 0, mine), lg, first_first).astype(BF16)


def place_kernel(odd, near, last_near, last_far, far, *refs):
    outs, held, sems = refs[:2], refs[2:4], refs[4]
    tokens, width = held[0].shape
    step = width // 4
    place = lax.broadcasted_iota(jnp.int32, (tokens, tokens), 0).astype(F32)
    order = (place == last_far[:1, width:].astype(F32)).astype(F32).astype(BF16)
    select = last_near[:, width:]
    for c in range(4):
        cols = slice(c * step, (c + 1) * step)
        held[0][:, cols] = (
            near[:, cols].astype(F32) + dot(select, last_near[:, cols], first_first)
        ).astype(BF16)
        rows = jnp.concatenate([last_far[:, cols], far[:, cols]])
        held[1][:, cols] = dot(order, rows, first_first).astype(BF16)
        for k, block in enumerate(held):
            for out, from_odd in ((outs[0], k == 0), (outs[1], k == 1)):

                @pl.when((odd[0] == 1) == from_odd)
                def _(out=out, block=block, k=k, cols=cols):
                    pltpu.make_async_copy(block.at[:, cols], out.at[:, cols], sems.at[k]).start()

    for k, block in enumerate(held):
        pltpu.make_async_copy(block, outs[k], sems.at[k]).wait()


def placed(odd, near, last_near, last_far, far):
    tokens, width = near.shape
    return call(
        place_kernel,
        [((tokens, width), BF16)] * 2,
        (odd, near, last_near, last_far, far),
        in_specs=[scalar] + [whole] * 4,
        out_specs=[outside] * 2,
        scratch_shapes=[pltpu.VMEM((tokens, width), BF16)] * 2 + [pltpu.SemaphoreType.DMA((2,))],
    )


def on_device(section_in_a, route_a, router, gate_up, down_proj, section_in_b, route_b, grad_out_b):
    groups = lax.axis_size("expert")
    pipe = lax.axis_size("pipe")
    me = lax.axis_index("expert")
    wsplit = min(8, groups)
    flight = groups // wsplit
    mine = me // wsplit
    tok_rows, width = section_in_a.shape[1:]
    topk = route_a.shape[2]
    slot_count = tok_rows // 8
    slots = flight * slot_count
    router_table = router[0]
    experts = router_table.shape[1]
    hidden_width = gate_up.shape[3]
    bits = [1 << k for k in reversed(range(groups.bit_length() - 1))]

    odd = lax.axis_index("pipe") % 2
    packed, twin_rows, sel_a, sel_b, to_near = call(
        functools.partial(pick_kernel, flight, slot_count, topk),
        [
            ((3, slots, width + experts), BF16),
            ((2, slots, width), BF16),
            ((slots, tok_rows), BF16),
            ((slots, tok_rows), BF16),
            (section_in_a.shape, BF16),
        ],
        (odd.reshape(1), route_b[0].T, route_a[0].T, section_in_b[0], grad_out_b[0], section_in_a[0]),
        limit=61,
        in_specs=[scalar] + [outside] * 5,
        out_specs=[whole] * 4 + [outside],
        scratch_shapes=[pltpu.VMEM((topk, tok_rows), jnp.int32)] * 2
        + [pltpu.VMEM((tok_rows, width), BF16)] * 3
        + [pltpu.SemaphoreType.DMA((6,))],
    )

    first, at, to_far = call(
        functools.partial(order_kernel, flight, slots),
        [
            ((slots, width), BF16),
            ((slots, tok_rows), BF16),
            ((tok_rows - slots, width), BF16),
        ],
        (odd.reshape(1), route_a[0].T, route_b[0].T, section_in_a[0], grad_out_b[0]),
        limit=61,
        in_specs=[scalar] + [outside] * 4,
        out_specs=[whole] * 3,
        scratch_shapes=[
            pltpu.VMEM((topk, tok_rows), jnp.int32),
            pltpu.VMEM((tok_rows, width), BF16),
            pltpu.SemaphoreType.DMA((2,)),
        ],
    )

    def everywhere(block):
        pieces = [block]
        for bit in bits:
            pieces += [exchanged(piece, bit) for piece in pieces]
        return pieces

    def of_mine(piece):
        if flight == 1:
            return piece
        split = piece.reshape(piece.shape[0], flight, slot_count, piece.shape[2])
        return lax.dynamic_index_in_dim(split, mine, axis=1, keepdims=False)

    def spread(values):
        if flight == 1:
            return values
        here = (jnp.arange(flight) == mine)[:, None, None]
        full = jnp.where(here, values[..., None, :, :], jnp.zeros((), values.dtype))
        return full.reshape(values.shape[:-2] + (slots, values.shape[-1]))

    own_all = everywhere(packed)
    from_near = lax.ppermute(to_near, "pipe", near(pipe))[0]
    from_far = lax.ppermute(to_far, "pipe", far(pipe))
    twin_all = everywhere(lax.ppermute(twin_rows, "pipe", twins(pipe)))
    twin = [of_mine(p) for p in twin_all]
    own = [of_mine(p) for p in own_all]
    rows_all = groups * slot_count
    lanes = 2 * width + 128

    *parts, basis, factors = call(
        functools.partial(expert_kernel, groups, topk),
        [((slot_count, lanes), BF16)] * groups
        + [((groups, slot_count, experts), F32), ((rows_all, 3 * hidden_width), BF16)],
        (mine.reshape(1), *own, router_table, gate_up[0], down_proj[0]),
        in_specs=[scalar] + [whole] * (groups + 3),
        out_specs=[whole] * (groups + 2),
        scratch_shapes=[
            pltpu.VMEM((2 * rows_all, width), BF16),
            pltpu.VMEM((rows_all, width), BF16),
            pltpu.VMEM((2 * rows_all, experts), F32),
        ],
    )
    if flight > 1:
        held = jnp.concatenate([piece[0] for piece in own_all]).reshape(groups * slots, -1)
        named = jnp.tile(jnp.repeat(jnp.arange(flight), slot_count), groups)
        basis = gates(
            held[:, width:].astype(F32),
            dot(held[:, :width], router_table),
            topk,
            named.astype(F32)[:, None],
        )[1].reshape(groups, slots, experts)
    terms = [[spread(part)] for part in parts]
    span, carrier = groups, terms[0][0]
    for bit in reversed(bits):
        sums = [terms[j][0] for j in range(span // 2, span)]
        split = span == 2
        if span < groups:
            sizes = [len(terms[j]) for j in range(span // 2, span)]
            given = [term for j in range(span // 2, span) for term in terms[j]]
            sums = call(
                functools.partial(middle_kernel, groups, span, sizes, split),
                [((slots, width), BF16), ((slots, width + 128), BF16)]
                if split
                else [((slots, lanes), BF16)] * len(sizes),
                (carrier, terms[span - 1][-1], *given, *twin_all),
                in_specs=[whole] * (2 + len(given)) + [anywhere] * groups,
                out_specs=[whole] * (2 if split else len(sizes)),
            )
            carrier = sums[-1]
        span //= 2
        if split:
            terms[0] += [exchanged(value, bit) for value in sums]
        else:
            for j in reversed(range(span)):
                terms[j].append(exchanged(sums[j], bit))
    last_near, last_far, wide = call(
        functools.partial(last_kernel, groups, span, len(terms[0])),
        [
            ((slots, width + tok_rows), BF16),
            ((slots, width + tok_rows), BF16),
            ((groups, slot_count, 3 * hidden_width + flight * experts), BF16),
        ],
        (
            odd.reshape(1),
            carrier,
            *terms[0],
            basis,
            router_table,
            factors,
            sel_a,
            sel_b,
            first,
            at,
        ),
        in_specs=[scalar] + [whole] * (len(terms[0]) + 8),
        out_specs=[whole] * 3,
    )
    twin_wide = lax.ppermute(wide, "pipe", twins(pipe))
    last_near = lax.ppermute(last_near, "pipe", near(pipe))
    last_far = lax.ppermute(last_far, "pipe", far(pipe))

    share = width // groups
    tiles = min(8, share // 128)
    tile = width // tiles
    same = flight == 1
    held = (*own, *twin) if same else (*own, *twin, *own_all, *twin_all)
    grad_gate_up, grad_down, grad_router = call(
        functools.partial(grads_kernel, groups, hidden_width, experts, same),
        [
            ((2, width, hidden_width), BF16),
            ((hidden_width, width), BF16),
            ((share, experts), BF16),
        ],
        (me.reshape(1), *held, wide, twin_wide),
        grid=(tiles,),
        in_specs=[scalar] + [whole] * (len(held) + 2),
        out_specs=[
            pl.BlockSpec((2, tile, hidden_width), lambda i: (0, i, 0)),
            pl.BlockSpec((hidden_width, tile), lambda i: (0, i)),
            pl.BlockSpec((share // tiles, experts), lambda i: (i, 0)),
        ],
    )
    section_out_a, grad_in_b = placed(odd.reshape(1), from_near, last_near, last_far, from_far)
    return (
        section_out_a[None],
        grad_in_b[None],
        grad_gate_up[None],
        grad_down[None],
        grad_router[None],
    )


def solution(mesh):
    return jax.shard_map(
        on_device,
        mesh=mesh,
        in_specs=(
            P("pipe", "expert", None),
            P("pipe", "expert", None),
            P("pipe", None, None),
            P("pipe", None, None, "expert"),
            P("pipe", "expert", None),
            P("pipe", "expert", None),
            P("pipe", "expert", None),
            P("pipe", "expert", None),
        ),
        out_specs=(
            P("pipe", "expert", None),
            P("pipe", "expert", None),
            P("pipe", None, None, "expert"),
            P("pipe", "expert", None),
            P("pipe", "expert", None),
        ),
        check_vma=False,
    )
```

```python
import functools

import jax
import jax.numpy as jnp
from jax import lax
from jax.experimental import pallas as pl
from jax.experimental.pallas import tpu as pltpu
from jax.sharding import PartitionSpec as P

F32, BF16 = jnp.float32, jnp.bfloat16
whole = pl.BlockSpec(memory_space=pltpu.VMEM)
anywhere = pl.BlockSpec(memory_space=pl.ANY)
outside = pl.BlockSpec(memory_space=pltpu.HBM)
scalar = pl.BlockSpec(memory_space=pltpu.SMEM)
last_last = (((1,), (1,)), ((), ()))
first_first = (((0,), (0,)), ((), ()))
MIB = 1 << 20


def dot(a, b, dims=(((1,), (0,)), ((), ()))):
    return lax.dot_general(a, b, dims, preferred_element_type=F32)


def near(count):
    return [(i, i ^ 1) for i in range(count)]


def far(count):
    return [(i, (i + 1 if i % 2 else i - 1) % count) for i in range(count)]


def twins(count):
    return [(i, count - 1 - i) for i in range(count)]


def exchanged(block, bit):
    count = lax.axis_size("expert")
    return lax.ppermute(block, "expert", [(i, i ^ bit) for i in range(count)])


def call(kernel, outs, args, limit=24, **more):
    return pl.pallas_call(
        kernel,
        out_shape=[jax.ShapeDtypeStruct(shape, dtype) for shape, dtype in outs],
        compiler_params=pltpu.CompilerParams(vmem_limit_bytes=limit * MIB),
        cost_estimate=pl.CostEstimate(flops=0, bytes_accessed=0, transcendentals=0),
        **more,
    )(*args)


def slot_select(ids, flight, slot_count):
    tokens = ids.shape[1]
    earlier = (
        lax.broadcasted_iota(jnp.int32, (tokens, tokens), 0)
        < lax.broadcasted_iota(jnp.int32, (tokens, tokens), 1)
    ).astype(F32).astype(BF16)
    slot_ids = lax.broadcasted_iota(jnp.int32, (slot_count, tokens), 0).astype(F32)
    picked = []
    for f in range(flight):
        named = jnp.max((ids == f).astype(F32), axis=0, keepdims=True)
        named = jnp.broadcast_to(named, (slot_count, tokens))
        rank = dot(named.astype(BF16), earlier)
        picked.append(jnp.where(rank == slot_ids, named, 0.0))
    return jnp.concatenate(picked, axis=0).astype(BF16)


def pick_kernel(flight, slot_count, topk, *refs):
    sources, refs = refs[:5], refs[5:]
    packed, twin, sel_a, sel_b = refs[:4]
    held, sems = refs[4:9], refs[9]
    copies = [
        pltpu.make_async_copy(source, here, sems.at[k])
        for k, (source, here) in enumerate(zip(sources, held))
    ]
    for copy in copies:
        copy.start()
    ids_b, ids_a, x_b, grad, x_a = held
    tokens, width = x_b.shape
    lanes = packed.shape[2] - width
    for k, (ids_ref, select_ref) in enumerate(((ids_b, sel_b), (ids_a, sel_a))):
        copies[k].wait()
        ids = ids_ref[...]
        select = slot_select(ids, flight, slot_count)
        select_ref[...] = select
        spare = jnp.zeros((lanes - topk, tokens), F32)
        numbers = jnp.concatenate([ids.astype(F32), spare], axis=0).astype(BF16)
        slot_ids = dot(select, numbers, last_last).astype(BF16)
        for place, source in ((0, 2), (1, 3)) if k == 0 else ((2, 4),):
            copies[source].wait()
            rows = dot(select, held[source][...]).astype(BF16)
            packed[place, :, :width] = rows
            packed[place, :, width:] = slot_ids
            if place < 2:
                twin[place] = rows


def order_kernel(flight, slots, sends_a, odd, ids_a, ids_b, x_a, grad, *refs):
    first, at, later, ids, block, sems = refs[-6:]
    for mine, ids_ref, block_ref in ((sends_a, ids_a, x_a), (1 - sends_a, ids_b, grad)):

        @pl.when(odd[0] == mine)
        def _(ids_ref=ids_ref, block_ref=block_ref):
            pltpu.make_async_copy(ids_ref, ids, sems.at[0]).start()
            pltpu.make_async_copy(block_ref, block, sems.at[1]).start()

    tokens = block.shape[0]
    earlier = (
        lax.broadcasted_iota(jnp.int32, (tokens, tokens), 0)
        < lax.broadcasted_iota(jnp.int32, (tokens, tokens), 1)
    ).astype(F32).astype(BF16)
    place = lax.broadcasted_iota(jnp.int32, (tokens, tokens), 0).astype(F32)
    token = lax.broadcasted_iota(jnp.int32, (8, tokens), 1).astype(F32)
    pltpu.make_async_copy(ids_a, ids, sems.at[0]).wait()
    named = jnp.max((ids[...] < flight).astype(F32), axis=0, keepdims=True)
    named = jnp.broadcast_to(named, (8, tokens))
    rank = dot(named.astype(BF16), earlier)
    count = jnp.sum(named, axis=1, keepdims=True)
    where = jnp.where(named > 0.0, rank, count + token - rank)[:1]
    at[...] = jnp.broadcast_to(where, at.shape).astype(BF16)
    order = (place == where).astype(F32).astype(BF16)
    pltpu.make_async_copy(x_a, block, sems.at[1]).wait()
    rows = dot(order, block[...]).astype(BF16)
    first[...] = rows[:slots, :]
    width = rows.shape[1]
    later[:, :width] = rows[slots:, :]
    if later.shape[1] > width:
        later[:, width:] = jnp.broadcast_to(where, (later.shape[0], tokens)).astype(BF16)


def gates(ids, logits, topk, expert):
    lanes = lax.broadcasted_iota(jnp.int32, logits.shape, 1).astype(F32)
    picks = [ids[:, k : k + 1] for k in range(topk)]
    chosen = [
        jnp.sum(jnp.where(lanes == pick, logits, 0.0), axis=1, keepdims=True) for pick in picks
    ]
    top = functools.reduce(jnp.maximum, chosen)
    powers = [jnp.exp(value - top) for value in chosen]
    scale = 1.0 / functools.reduce(jnp.add, powers)
    probs = [power * scale for power in powers]
    named = [(pick == expert).astype(F32) for pick in picks]
    weight = functools.reduce(jnp.add, [p * n for p, n in zip(probs, named)])
    basis = functools.reduce(
        jnp.add,
        [jnp.where(lanes == pick, p * (n - weight), 0.0) for pick, p, n in zip(picks, probs, named)],
    )
    return weight, basis


def coded(columns, lanes):
    rows = columns[0].shape[0]
    lane = lax.broadcasted_iota(jnp.int32, (rows, lanes), 1)
    out = jnp.zeros((rows, lanes), F32)
    for j, rest in enumerate(columns):
        for k in range(3):
            term = rest.astype(BF16).astype(F32)
            out = jnp.where(lane == 3 * j + k, term, out)
            rest = rest - term
    return out.astype(BF16)


def decoded(code, count):
    code = code.astype(F32)
    return [
        code[:, 3 * j : 3 * j + 1] + code[:, 3 * j + 1 : 3 * j + 2] + code[:, 3 * j + 2 : 3 * j + 3]
        for j in range(count)
    ]


def summed_scores(own, other, blocks, span, width):
    mine, theirs = decoded(own[:, width:], blocks), decoded(other[:, width:], blocks)
    return [mine[j] + theirs[j ^ span] for j in range(blocks)]


def expert_kernel(blocks, topk, mine, *refs):
    pieces, refs = refs[:blocks], refs[blocks:]
    (router, gate_up, down), refs = refs[:3], refs[3:]
    parts, refs = refs[:blocks], refs[blocks:]
    basis_out, factors, rows, grads, ids = refs
    slot_count = pieces[0].shape[1]
    width, hidden_width = gate_up.shape[1], gate_up.shape[2]
    half = blocks * slot_count
    for place in range(blocks):
        piece = pieces[place]
        here = pl.ds(place * slot_count, slot_count)
        there = pl.ds(half + place * slot_count, slot_count)
        rows[here, :] = piece[0, :, :width]
        rows[there, :] = piece[2, :, :width]
        grads[here, :] = piece[1, :, :width]
        ids[here, :] = piece[0, :, width:].astype(F32)
        ids[there, :] = piece[2, :, width:].astype(F32)
    weight, basis = gates(ids[...], dot(rows[...], router[...]), topk, mine[0].astype(F32))
    act_gate = dot(rows[...], gate_up[0])
    act_up = dot(rows[...], gate_up[1])
    back = dot(grads[...], down[...], last_last)
    logistic = jax.nn.sigmoid(act_gate)
    hidden = act_gate * logistic * act_up
    weight_b = weight[:half]
    hidden_b, gate_b, up_b, log_b = hidden[:half], act_gate[:half], act_up[:half], logistic[:half]
    basis_out[...] = basis[:half].reshape(basis_out.shape)
    scores = jnp.sum(hidden_b * back, axis=1, keepdims=True)
    code = coded(
        [scores[j * slot_count : (j + 1) * slot_count] for j in range(blocks)],
        parts[0].shape[1] - 2 * width,
    )
    d_hidden = weight_b * back
    d_gate = (d_hidden * up_b * log_b * (1.0 + gate_b * (1.0 - log_b))).astype(BF16)
    d_up = (d_hidden * gate_b * log_b).astype(BF16)
    factors[:, :hidden_width] = d_gate
    factors[:, hidden_width : 2 * hidden_width] = d_up
    factors[:, 2 * hidden_width :] = (weight_b * hidden_b).astype(BF16)
    hidden_a = (weight[half:] * hidden[half:]).astype(BF16)
    step = min(width, 512)
    for first in range(0, width, step):
        cols = slice(first, first + step)
        part_a = dot(hidden_a, down[:, cols]).astype(BF16)
        part_b = (
            dot(d_gate, gate_up[0, cols, :], last_last) + dot(d_up, gate_up[1, cols, :], last_last)
        ).astype(BF16)
        for j, part in enumerate(parts):
            here = slice(j * slot_count, (j + 1) * slot_count)
            part[:, cols] = part_a[here]
            part[:, first + width : first + width + step] = part_b[here]
    for part in parts:
        part[:, 2 * width :] = code


def added(terms, width):
    return functools.reduce(jnp.add, [term[:, :width].astype(F32) for term in terms])


def middle_kernel(blocks, span, sizes, split, own, other, *refs):
    terms, outs = refs[: sum(sizes)], refs[sum(sizes) + blocks :]
    lanes = own.shape[1] - 128
    code = coded(summed_scores(own, other, blocks, span, lanes), 128)
    for size in sizes:
        total = added(terms[:size], lanes).astype(BF16)
        if split:
            outs[0][...] = total[:, : lanes // 2]
            outs[1][:, : lanes // 2] = total[:, lanes // 2 :]
            outs[1][:, lanes // 2 :] = code
        else:
            outs[0][:, :lanes] = total
            outs[0][:, lanes:] = code
            outs = outs[1:]
        terms = terms[size:]


def last_kernel(blocks, span, count, odd, own, *refs):
    terms, refs = refs[: count - 2], refs[count - 2 :]
    last_a, last_b, basis, router, factors, sel_a, sel_b = refs[:7]
    first_near, first_far, at_near, at_far, to_near, to_far, wide = refs[7:]
    width, experts = router.shape
    slots = first_near.shape[0]
    total = added(terms, 2 * width)
    scores = summed_scores(own, last_b, blocks, span, width)
    sums = [(score * basis[j]).astype(BF16) for j, score in enumerate(scores)]
    more_a = total[:, :width] + last_a[...].astype(F32)
    more_b = (
        total[:, width:] + last_b[:, :width].astype(F32) + dot(sums[0], router[...], last_last)
    )
    even = odd[0] == 0
    for sends_a, first, at, out in (
        (even, first_near, at_near, to_near),
        (jnp.logical_not(even), first_far, at_far, to_far),
    ):
        more = jnp.where(sends_a, more_a, more_b)
        if slots * blocks != factors.shape[0]:
            place = lax.broadcasted_iota(jnp.int32, at.shape, 0).astype(F32)
            row = (place == at[...].astype(F32)).astype(F32).astype(BF16)
            slot = jnp.where(sends_a, sel_a[...].astype(F32), sel_b[...].astype(F32)).astype(BF16)
            more = jnp.dot(dot(row, slot, last_last), more, precision=lax.Precision.HIGHEST)
        out[:, :width] = (first[...].astype(F32) + more).astype(BF16)
        if out.shape[1] > width:
            out[:, width:] = at[...]
    slot_count = factors.shape[0] // blocks
    core = factors.shape[1]
    for j, value in enumerate(sums):
        wide[j, :, :core] = factors[j * slot_count : (j + 1) * slot_count, :]
        for f in range(value.shape[0] // slot_count):
            wide[j, :, core + f * experts : core + (f + 1) * experts] = value[
                f * slot_count : (f + 1) * slot_count
            ]


def grads_kernel(blocks, hidden_width, experts, same, me, *refs):
    pieces, refs = refs[: 2 * blocks], refs[2 * blocks :]
    pieces_all = pieces
    if not same:
        pieces_all, refs = refs[: 2 * blocks], refs[2 * blocks :]
    own_wide, twin_wide, gate_up, down, router = refs
    i = pl.program_id(0)
    tile, share_tile = down.shape[1], router.shape[0]
    share = share_tile * pl.num_programs(0)
    cols = pl.ds(pl.multiple_of(i * tile, tile), tile)
    mine = pl.ds(pl.multiple_of(me[0] * share + i * share_tile, 128), share_tile)

    def stacked(held, which, where):
        return jnp.concatenate([piece[which, :, where] for piece in held])

    def column(first, size):
        return jnp.concatenate(
            [w[j, :, first : first + size] for w in (own_wide, twin_wide) for j in range(blocks)]
        )

    core = 3 * hidden_width
    both = dot(stacked(pieces, 0, cols), column(0, 2 * hidden_width), first_first).astype(BF16)
    gate_up[0] = both[:, :hidden_width]
    gate_up[1] = both[:, hidden_width:]
    down[...] = dot(
        column(2 * hidden_width, hidden_width), stacked(pieces, 1, cols), first_first
    ).astype(BF16)
    flight = (own_wide.shape[2] - core) // experts
    lg = jnp.concatenate(
        [
            w[j, :, core + f * experts : core + (f + 1) * experts]
            for w in (own_wide, twin_wide)
            for j in range(blocks)
            for f in range(flight)
        ]
    )
    router[...] = dot(stacked(pieces_all, 0, mine), lg, first_first).astype(BF16)


def place_kernel(odd, last_near, near, last_far, far, *refs):
    outs, held, sems = refs[:2], refs[2:4], refs[4]
    tokens, width = held[0].shape
    step = width // 4
    place = lax.broadcasted_iota(jnp.int32, (tokens, tokens), 0).astype(F32)
    orders = [
        (place == at[:1, width:].astype(F32)).astype(F32).astype(BF16) for at in (near, last_far)
    ]
    for c in range(4):
        cols = slice(c * step, (c + 1) * step)
        for k, (last, later) in enumerate(((last_near, near), (last_far, far))):
            rows = jnp.concatenate([last[:, cols], later[:, cols]])
            held[k][:, cols] = dot(orders[k], rows, first_first).astype(BF16)
            for out, from_odd in ((outs[0], k == 0), (outs[1], k == 1)):

                @pl.when((odd[0] == 1) == from_odd)
                def _(out=out, k=k, cols=cols):
                    pltpu.make_async_copy(
                        held[k].at[:, cols], out.at[:, cols], sems.at[k]
                    ).start()

    for k, block in enumerate(held):
        pltpu.make_async_copy(block, outs[k], sems.at[k]).wait()


def placed(odd, last_near, near, last_far, far):
    tokens, width = far.shape[0] + last_far.shape[0], far.shape[1]
    return call(
        place_kernel,
        [((tokens, width), BF16)] * 2,
        (odd, last_near, near, last_far, far),
        in_specs=[scalar] + [whole] * 4,
        out_specs=[outside] * 2,
        scratch_shapes=[pltpu.VMEM((tokens, width), BF16)] * 2 + [pltpu.SemaphoreType.DMA((2,))],
    )


def on_device(section_in_a, route_a, router, gate_up, down_proj, section_in_b, route_b, grad_out_b):
    groups = lax.axis_size("expert")
    pipe = lax.axis_size("pipe")
    me = lax.axis_index("expert")
    wsplit = min(8, groups)
    flight = groups // wsplit
    mine = me // wsplit
    tok_rows, width = section_in_a.shape[1:]
    topk = route_a.shape[2]
    slot_count = tok_rows // 8
    slots = flight * slot_count
    router_table = router[0]
    experts = router_table.shape[1]
    hidden_width = gate_up.shape[3]
    bits = [1 << k for k in reversed(range(groups.bit_length() - 1))]

    odd = lax.axis_index("pipe") % 2
    packed, twin_rows, sel_a, sel_b = call(
        functools.partial(pick_kernel, flight, slot_count, topk),
        [
            ((3, slots, width + experts), BF16),
            ((2, slots, width), BF16),
            ((slots, tok_rows), BF16),
            ((slots, tok_rows), BF16),
        ],
        (route_b[0].T, route_a[0].T, section_in_b[0], grad_out_b[0], section_in_a[0]),
        limit=61,
        in_specs=[outside] * 5,
        out_specs=[whole] * 4,
        scratch_shapes=[pltpu.VMEM((topk, tok_rows), jnp.int32)] * 2
        + [pltpu.VMEM((tok_rows, width), BF16)] * 3
        + [pltpu.SemaphoreType.DMA((5,))],
    )

    def ordered(sends_a, lanes, after):
        return call(
            functools.partial(order_kernel, flight, slots, sends_a),
            [
                ((slots, width), BF16),
                ((slots, tok_rows), BF16),
                ((tok_rows - slots, width + lanes), BF16),
            ],
            (odd.reshape(1), route_a[0].T, route_b[0].T, section_in_a[0], grad_out_b[0], *after),
            limit=61,
            in_specs=[scalar] + [outside] * 4 + [anywhere] * len(after),
            out_specs=[whole] * 3,
            scratch_shapes=[
                pltpu.VMEM((topk, tok_rows), jnp.int32),
                pltpu.VMEM((tok_rows, width), BF16),
                pltpu.SemaphoreType.DMA((2,)),
            ],
        )

    def everywhere(block):
        pieces = [block]
        for bit in bits:
            pieces += [exchanged(piece, bit) for piece in pieces]
        return pieces

    def of_mine(piece):
        if flight == 1:
            return piece
        split = piece.reshape(piece.shape[0], flight, slot_count, piece.shape[2])
        return lax.dynamic_index_in_dim(split, mine, axis=1, keepdims=False)

    def spread(values):
        if flight == 1:
            return values
        here = (jnp.arange(flight) == mine)[:, None, None]
        full = jnp.where(here, values[..., None, :, :], jnp.zeros((), values.dtype))
        return full.reshape(values.shape[:-2] + (slots, values.shape[-1]))

    own_all = everywhere(packed)
    first_near, at_near, to_near = ordered(0, tok_rows, ())
    from_near = lax.ppermute(to_near, "pipe", near(pipe))
    first_far, at_far, to_far = ordered(1, 0, own_all[1:2])
    from_far = lax.ppermute(to_far, "pipe", far(pipe))
    twin_all = everywhere(lax.ppermute(twin_rows, "pipe", twins(pipe)))
    twin = [of_mine(p) for p in twin_all]
    own = [of_mine(p) for p in own_all]
    rows_all = groups * slot_count
    lanes = 2 * width + 128

    *parts, basis, factors = call(
        functools.partial(expert_kernel, groups, topk),
        [((slot_count, lanes), BF16)] * groups
        + [((groups, slot_count, experts), F32), ((rows_all, 3 * hidden_width), BF16)],
        (mine.reshape(1), *own, router_table, gate_up[0], down_proj[0]),
        in_specs=[scalar] + [whole] * (groups + 3),
        out_specs=[whole] * (groups + 2),
        scratch_shapes=[
            pltpu.VMEM((2 * rows_all, width), BF16),
            pltpu.VMEM((rows_all, width), BF16),
            pltpu.VMEM((2 * rows_all, experts), F32),
        ],
    )
    if flight > 1:
        held = jnp.concatenate([piece[0] for piece in own_all]).reshape(groups * slots, -1)
        named = jnp.tile(jnp.repeat(jnp.arange(flight), slot_count), groups)
        basis = gates(
            held[:, width:].astype(F32),
            dot(held[:, :width], router_table),
            topk,
            named.astype(F32)[:, None],
        )[1].reshape(groups, slots, experts)
    terms = [[spread(part)] for part in parts]
    span, carrier = groups, terms[0][0]
    for bit in reversed(bits):
        sums = [terms[j][0] for j in range(span // 2, span)]
        split = span == 2
        if span < groups:
            sizes = [len(terms[j]) for j in range(span // 2, span)]
            given = [term for j in range(span // 2, span) for term in terms[j]]
            sums = call(
                functools.partial(middle_kernel, groups, span, sizes, split),
                [((slots, width), BF16), ((slots, width + 128), BF16)]
                if split
                else [((slots, lanes), BF16)] * len(sizes),
                (carrier, terms[span - 1][-1], *given, *twin_all),
                in_specs=[whole] * (2 + len(given)) + [anywhere] * groups,
                out_specs=[whole] * (2 if split else len(sizes)),
            )
            carrier = sums[-1]
        span //= 2
        if split:
            terms[0] += [exchanged(value, bit) for value in sums]
        else:
            for j in reversed(range(span)):
                terms[j].append(exchanged(sums[j], bit))
    last_near, last_far, wide = call(
        functools.partial(last_kernel, groups, span, len(terms[0])),
        [
            ((slots, width), BF16),
            ((slots, width + tok_rows), BF16),
            ((groups, slot_count, 3 * hidden_width + flight * experts), BF16),
        ],
        (
            odd.reshape(1),
            carrier,
            *terms[0],
            basis,
            router_table,
            factors,
            sel_a,
            sel_b,
            first_near,
            first_far,
            at_near,
            at_far,
        ),
        in_specs=[scalar] + [whole] * (len(terms[0]) + 10),
        out_specs=[whole] * 3,
    )
    twin_wide = lax.ppermute(wide, "pipe", twins(pipe))
    last_near = lax.ppermute(last_near, "pipe", near(pipe))
    last_far = lax.ppermute(last_far, "pipe", far(pipe))

    share = width // groups
    tiles = min(8, share // 128)
    tile = width // tiles
    same = flight == 1
    held = (*own, *twin) if same else (*own, *twin, *own_all, *twin_all)
    grad_gate_up, grad_down, grad_router = call(
        functools.partial(grads_kernel, groups, hidden_width, experts, same),
        [
            ((2, width, hidden_width), BF16),
            ((hidden_width, width), BF16),
            ((share, experts), BF16),
        ],
        (me.reshape(1), *held, wide, twin_wide),
        grid=(tiles,),
        in_specs=[scalar] + [whole] * (len(held) + 2),
        out_specs=[
            pl.BlockSpec((2, tile, hidden_width), lambda i: (0, i, 0)),
            pl.BlockSpec((hidden_width, tile), lambda i: (0, i)),
            pl.BlockSpec((share // tiles, experts), lambda i: (i, 0)),
        ],
    )
    section_out_a, grad_in_b = placed(odd.reshape(1), last_near, from_near, last_far, from_far)
    return (
        section_out_a[None],
        grad_in_b[None],
        grad_gate_up[None],
        grad_down[None],
        grad_router[None],
    )


def solution(mesh):
    return jax.shard_map(
        on_device,
        mesh=mesh,
        in_specs=(
            P("pipe", "expert", None),
            P("pipe", "expert", None),
            P("pipe", None, None),
            P("pipe", None, None, "expert"),
            P("pipe", "expert", None),
            P("pipe", "expert", None),
            P("pipe", "expert", None),
            P("pipe", "expert", None),
        ),
        out_specs=(
            P("pipe", "expert", None),
            P("pipe", "expert", None),
            P("pipe", None, None, "expert"),
            P("pipe", "expert", None),
            P("pipe", "expert", None),
        ),
        check_vma=False,
    )
```

```python
import functools

import jax
import jax.numpy as jnp
from jax import lax
from jax.experimental import pallas as pl
from jax.experimental.pallas import tpu as pltpu
from jax.sharding import PartitionSpec as P

F32, BF16 = jnp.float32, jnp.bfloat16
whole = pl.BlockSpec(memory_space=pltpu.VMEM)
anywhere = pl.BlockSpec(memory_space=pl.ANY)
outside = pl.BlockSpec(memory_space=pltpu.HBM)
scalar = pl.BlockSpec(memory_space=pltpu.SMEM)
last_last = (((1,), (1,)), ((), ()))
first_first = (((0,), (0,)), ((), ()))
MIB = 1 << 20


def dot(a, b, dims=(((1,), (0,)), ((), ()))):
    return lax.dot_general(a, b, dims, preferred_element_type=F32)


def near(count):
    return [(i, i ^ 1) for i in range(count)]


def far(count):
    return [(i, (i + 1 if i % 2 else i - 1) % count) for i in range(count)]


def twins(count):
    return [(i, count - 1 - i) for i in range(count)]


def exchanged(block, bit):
    count = lax.axis_size("expert")
    return lax.ppermute(block, "expert", [(i, i ^ bit) for i in range(count)])


def call(kernel, outs, args, limit=24, **more):
    return pl.pallas_call(
        kernel,
        out_shape=[jax.ShapeDtypeStruct(shape, dtype) for shape, dtype in outs],
        compiler_params=pltpu.CompilerParams(vmem_limit_bytes=limit * MIB),
        cost_estimate=pl.CostEstimate(flops=0, bytes_accessed=0, transcendentals=0),
        **more,
    )(*args)


def slot_select(ids, flight, slot_count):
    tokens = ids.shape[1]
    earlier = (
        lax.broadcasted_iota(jnp.int32, (tokens, tokens), 0)
        < lax.broadcasted_iota(jnp.int32, (tokens, tokens), 1)
    ).astype(F32).astype(BF16)
    slot_ids = lax.broadcasted_iota(jnp.int32, (slot_count, tokens), 0).astype(F32)
    picked = []
    for f in range(flight):
        named = jnp.max((ids == f).astype(F32), axis=0, keepdims=True)
        named = jnp.broadcast_to(named, (slot_count, tokens))
        rank = dot(named.astype(BF16), earlier)
        picked.append(jnp.where(rank == slot_ids, named, 0.0))
    return jnp.concatenate(picked, axis=0).astype(BF16)


def pick_kernel(flight, slot_count, topk, *refs):
    sources, refs = refs[:5], refs[5:]
    packed, twin, sel_a, sel_b = refs[:4]
    held, sems = refs[4:9], refs[9]
    copies = [
        pltpu.make_async_copy(source, here, sems.at[k])
        for k, (source, here) in enumerate(zip(sources, held))
    ]
    for copy in copies:
        copy.start()
    ids_b, ids_a, x_b, grad, x_a = held
    tokens, width = x_b.shape
    lanes = packed.shape[2] - width
    for k, (ids_ref, select_ref) in enumerate(((ids_b, sel_b), (ids_a, sel_a))):
        copies[k].wait()
        ids = ids_ref[...]
        select = slot_select(ids, flight, slot_count)
        select_ref[...] = select
        spare = jnp.zeros((lanes - topk, tokens), F32)
        numbers = jnp.concatenate([ids.astype(F32), spare], axis=0).astype(BF16)
        slot_ids = dot(select, numbers, last_last).astype(BF16)
        for place, source in ((0, 2), (1, 3)) if k == 0 else ((2, 4),):
            copies[source].wait()
            rows = dot(select, held[source][...]).astype(BF16)
            packed[place, :, :width] = rows
            packed[place, :, width:] = slot_ids
            if place < 2:
                twin[place] = rows


def order_kernel(flight, slots, sends_a, odd, ids_a, ids_b, x_a, grad, *refs):
    first, at, later, ids, block, sems = refs[-6:]
    for mine, ids_ref, block_ref in ((sends_a, ids_a, x_a), (1 - sends_a, ids_b, grad)):

        @pl.when(odd[0] == mine)
        def _(ids_ref=ids_ref, block_ref=block_ref):
            pltpu.make_async_copy(ids_ref, ids, sems.at[0]).start()
            pltpu.make_async_copy(block_ref, block, sems.at[1]).start()

    tokens = block.shape[0]
    earlier = (
        lax.broadcasted_iota(jnp.int32, (tokens, tokens), 0)
        < lax.broadcasted_iota(jnp.int32, (tokens, tokens), 1)
    ).astype(F32).astype(BF16)
    place = lax.broadcasted_iota(jnp.int32, (tokens, tokens), 0).astype(F32)
    token = lax.broadcasted_iota(jnp.int32, (8, tokens), 1).astype(F32)
    pltpu.make_async_copy(ids_a, ids, sems.at[0]).wait()
    named = jnp.max((ids[...] < flight).astype(F32), axis=0, keepdims=True)
    named = jnp.broadcast_to(named, (8, tokens))
    rank = dot(named.astype(BF16), earlier)
    count = jnp.sum(named, axis=1, keepdims=True)
    where = jnp.where(named > 0.0, rank, count + token - rank)[:1]
    at[...] = jnp.broadcast_to(where, at.shape).astype(BF16)
    order = (place == where).astype(F32).astype(BF16)
    pltpu.make_async_copy(x_a, block, sems.at[1]).wait()
    rows = dot(order, block[...]).astype(BF16)
    first[...] = rows[:slots, :]
    width = rows.shape[1]
    later[:, :width] = rows[slots:, :]
    spare = later.shape[1] - width
    if spare == tokens:
        later[:, width:] = jnp.broadcast_to(where, (later.shape[0], tokens)).astype(BF16)
    else:
        row = lax.broadcasted_iota(jnp.int32, (later.shape[0], spare), 0)
        halves = [where[:, k * spare : (k + 1) * spare] for k in (0, 1)]
        later[:, width:] = jnp.where(row % 2 == 0, halves[0], halves[1]).astype(BF16)


def gates(ids, logits, topk, expert):
    lanes = lax.broadcasted_iota(jnp.int32, logits.shape, 1).astype(F32)
    picks = [ids[:, k : k + 1] for k in range(topk)]
    chosen = [
        jnp.sum(jnp.where(lanes == pick, logits, 0.0), axis=1, keepdims=True) for pick in picks
    ]
    top = functools.reduce(jnp.maximum, chosen)
    powers = [jnp.exp(value - top) for value in chosen]
    scale = 1.0 / functools.reduce(jnp.add, powers)
    probs = [power * scale for power in powers]
    named = [(pick == expert).astype(F32) for pick in picks]
    weight = functools.reduce(jnp.add, [p * n for p, n in zip(probs, named)])
    basis = functools.reduce(
        jnp.add,
        [jnp.where(lanes == pick, p * (n - weight), 0.0) for pick, p, n in zip(picks, probs, named)],
    )
    return weight, basis


def coded(columns, lanes):
    rows = columns[0].shape[0]
    lane = lax.broadcasted_iota(jnp.int32, (rows, lanes), 1)
    out = jnp.zeros((rows, lanes), F32)
    for j, rest in enumerate(columns):
        for k in range(3):
            term = rest.astype(BF16).astype(F32)
            out = jnp.where(lane == 3 * j + k, term, out)
            rest = rest - term
    return out.astype(BF16)


def decoded(code, count):
    code = code.astype(F32)
    return [
        code[:, 3 * j : 3 * j + 1] + code[:, 3 * j + 1 : 3 * j + 2] + code[:, 3 * j + 2 : 3 * j + 3]
        for j in range(count)
    ]


def summed_scores(own, other, blocks, span, width):
    mine, theirs = decoded(own[:, width:], blocks), decoded(other[:, width:], blocks)
    return [mine[j] + theirs[j ^ span] for j in range(blocks)]


def expert_kernel(blocks, topk, mine, *refs):
    pieces, refs = refs[:blocks], refs[blocks:]
    sources, refs = refs[:3], refs[3:]
    parts, refs = refs[:blocks], refs[blocks:]
    basis_out, factors, rows, grads, ids, router, gate_up, down, sems = refs
    copies = [
        pltpu.make_async_copy(source, here, sems.at[k])
        for k, (source, here) in enumerate(
            (
                (sources[1].at[0], gate_up.at[0]),
                (sources[1].at[1], gate_up.at[1]),
                (sources[2], down),
                (sources[0], router),
            )
        )
    ]
    for copy in copies:
        copy.start()
    slot_count = pieces[0].shape[1]
    width, hidden_width = gate_up.shape[1], gate_up.shape[2]
    half = blocks * slot_count
    for place in range(blocks):
        piece = pieces[place]
        here = pl.ds(place * slot_count, slot_count)
        there = pl.ds(half + place * slot_count, slot_count)
        rows[here, :] = piece[0, :, :width]
        rows[there, :] = piece[2, :, :width]
        grads[here, :] = piece[1, :, :width]
        ids[here, :] = piece[0, :, width:].astype(F32)
        ids[there, :] = piece[2, :, width:].astype(F32)
    copies[0].wait()
    act_gate = dot(rows[...], gate_up[0])
    copies[1].wait()
    act_up = dot(rows[...], gate_up[1])
    copies[2].wait()
    back = dot(grads[...], down[...], last_last)
    copies[3].wait()
    weight, basis = gates(ids[...], dot(rows[...], router[...]), topk, mine[0].astype(F32))
    logistic = jax.nn.sigmoid(act_gate)
    hidden = act_gate * logistic * act_up
    weight_b = weight[:half]
    hidden_b, gate_b, up_b, log_b = hidden[:half], act_gate[:half], act_up[:half], logistic[:half]
    basis_out[...] = basis[:half].reshape(basis_out.shape)
    scores = jnp.sum(hidden_b * back, axis=1, keepdims=True)
    code = coded(
        [scores[j * slot_count : (j + 1) * slot_count] for j in range(blocks)],
        parts[0].shape[1] - 2 * width,
    )
    d_hidden = weight_b * back
    d_gate = (d_hidden * up_b * log_b * (1.0 + gate_b * (1.0 - log_b))).astype(BF16)
    d_up = (d_hidden * gate_b * log_b).astype(BF16)
    factors[:, :hidden_width] = d_gate
    factors[:, hidden_width : 2 * hidden_width] = d_up
    factors[:, 2 * hidden_width :] = (weight_b * hidden_b).astype(BF16)
    hidden_a = (weight[half:] * hidden[half:]).astype(BF16)
    step = min(width, 512)
    for first in range(0, width, step):
        cols = slice(first, first + step)
        part_a = dot(hidden_a, down[:, cols]).astype(BF16)
        part_b = (
            dot(d_gate, gate_up[0, cols, :], last_last) + dot(d_up, gate_up[1, cols, :], last_last)
        ).astype(BF16)
        for j, part in enumerate(parts):
            here = slice(j * slot_count, (j + 1) * slot_count)
            part[:, cols] = part_a[here]
            part[:, first + width : first + width + step] = part_b[here]
    for part in parts:
        part[:, 2 * width :] = code


def added(terms, width):
    return functools.reduce(jnp.add, [term[:, :width].astype(F32) for term in terms])


def middle_kernel(blocks, span, sizes, split, own, other, *refs):
    terms, outs = refs[: sum(sizes)], refs[sum(sizes) + blocks :]
    lanes = own.shape[1] - 128
    code = coded(summed_scores(own, other, blocks, span, lanes), 128)
    for size in sizes:
        total = added(terms[:size], lanes).astype(BF16)
        if split:
            outs[0][...] = total[:, : lanes // 2]
            outs[1][:, : lanes // 2] = total[:, lanes // 2 :]
            outs[1][:, lanes // 2 :] = code
        else:
            outs[0][:, :lanes] = total
            outs[0][:, lanes:] = code
            outs = outs[1:]
        terms = terms[size:]


def last_kernel(blocks, span, count, odd, own, *refs):
    terms, refs = refs[: count - 2], refs[count - 2 :]
    last_a, last_b, basis, router, factors, sel_a, sel_b = refs[:7]
    first_near, first_far, at_near, at_far, to_near, to_far, wide = refs[7:]
    width, experts = router.shape
    slots = first_near.shape[0]
    total = added(terms, 2 * width)
    scores = summed_scores(own, last_b, blocks, span, width)
    sums = [(score * basis[j]).astype(BF16) for j, score in enumerate(scores)]
    more_a = total[:, :width] + last_a[...].astype(F32)
    more_b = (
        total[:, width:] + last_b[:, :width].astype(F32) + dot(sums[0], router[...], last_last)
    )
    even = odd[0] == 0
    for sends_a, first, at, out in (
        (even, first_near, at_near, to_near),
        (jnp.logical_not(even), first_far, at_far, to_far),
    ):
        more = jnp.where(sends_a, more_a, more_b)
        if slots * blocks != factors.shape[0]:
            place = lax.broadcasted_iota(jnp.int32, at.shape, 0).astype(F32)
            row = (place == at[...].astype(F32)).astype(F32).astype(BF16)
            slot = jnp.where(sends_a, sel_a[...].astype(F32), sel_b[...].astype(F32)).astype(BF16)
            more = jnp.dot(dot(row, slot, last_last), more, precision=lax.Precision.HIGHEST)
        out[:, :width] = (first[...].astype(F32) + more).astype(BF16)
        if out.shape[1] > width:
            out[:, width:] = at[...]
    slot_count = factors.shape[0] // blocks
    core = factors.shape[1]
    for j, value in enumerate(sums):
        wide[j, :, :core] = factors[j * slot_count : (j + 1) * slot_count, :]
        for f in range(value.shape[0] // slot_count):
            wide[j, :, core + f * experts : core + (f + 1) * experts] = value[
                f * slot_count : (f + 1) * slot_count
            ]


def grads_kernel(blocks, hidden_width, experts, same, me, *refs):
    pieces, refs = refs[: 2 * blocks], refs[2 * blocks :]
    pieces_all = pieces
    if not same:
        pieces_all, refs = refs[: 2 * blocks], refs[2 * blocks :]
    own_wide, twin_wide, gate_up, down, router = refs
    i = pl.program_id(0)
    tile, share_tile = down.shape[1], router.shape[0]
    share = share_tile * pl.num_programs(0)
    cols = pl.ds(pl.multiple_of(i * tile, tile), tile)
    mine = pl.ds(pl.multiple_of(me[0] * share + i * share_tile, 128), share_tile)

    def stacked(held, which, where):
        return jnp.concatenate([piece[which, :, where] for piece in held])

    def column(first, size):
        return jnp.concatenate(
            [w[j, :, first : first + size] for w in (own_wide, twin_wide) for j in range(blocks)]
        )

    core = 3 * hidden_width
    both = dot(stacked(pieces, 0, cols), column(0, 2 * hidden_width), first_first).astype(BF16)
    gate_up[0] = both[:, :hidden_width]
    gate_up[1] = both[:, hidden_width:]
    down[...] = dot(
        column(2 * hidden_width, hidden_width), stacked(pieces, 1, cols), first_first
    ).astype(BF16)
    flight = (own_wide.shape[2] - core) // experts
    lg = jnp.concatenate(
        [
            w[j, :, core + f * experts : core + (f + 1) * experts]
            for w in (own_wide, twin_wide)
            for j in range(blocks)
            for f in range(flight)
        ]
    )
    router[...] = dot(stacked(pieces_all, 0, mine), lg, first_first).astype(BF16)


def order_of(places):
    tokens = places.shape[1]
    place = lax.broadcasted_iota(jnp.int32, (tokens, tokens), 0).astype(F32)
    return (place == places).astype(F32).astype(BF16)


def place_kernel(near, far, near_out, far_out, places):
    tokens, width = far_out.shape
    step = width // 4
    for k, (block, out) in enumerate(((near, near_out), (far, far_out))):
        spare = block.shape[1] - width
        if spare == tokens:
            at = block[:1, width:].astype(F32)
        else:
            rows = block[:16, width:]
            from_lane, to_lane = (
                lax.broadcasted_iota(jnp.int32, (spare, tokens), axis) for axis in (0, 1)
            )
            halves = [
                dot(rows, (to_lane == from_lane + h * spare).astype(F32).astype(BF16)) for h in (0, 1)
            ]
            at = halves[0][:1] + halves[1][1:2]
        places[k : k + 1] = at
        order = order_of(at)
        for c in range(4):
            cols = slice(c * step, (c + 1) * step)
            out[:, cols] = dot(order[tokens - block.shape[0] :], block[:, cols], first_first).astype(
                BF16
            )


def finish_kernel(odd, near, last_near, far, last_far, places, *refs):
    outs, held, sems = refs[:2], refs[2:4], refs[4]
    tokens, width = near.shape
    step = width // 4
    parts = (near, last_near), (far, last_far)
    orders = [order_of(places[k : k + 1])[: last.shape[0]] for k, (_, last) in enumerate(parts)]
    for c in range(4):
        cols = slice(c * step, (c + 1) * step)
        for k, (early, last) in enumerate(parts):
            late = dot(orders[k], last[:, cols], first_first)
            held[k][:, cols] = early[:, cols] + late.astype(BF16)
            for out, from_odd in ((outs[0], k == 0), (outs[1], k == 1)):

                @pl.when((odd[0] == 1) == from_odd)
                def _(out=out, k=k, cols=cols):
                    pltpu.make_async_copy(
                        held[k].at[:, cols], out.at[:, cols], sems.at[k]
                    ).start()

    for k, block in enumerate(held):
        pltpu.make_async_copy(block, outs[k], sems.at[k]).wait()


def placed(odd, last_near, near, last_far, far):
    slots, width = last_far.shape
    tokens = far.shape[0] + slots
    shape = ((tokens, width), BF16)
    early_near, early_far, places = call(
        place_kernel,
        [shape, shape, ((2, tokens), F32)],
        (near, far),
        in_specs=[whole] * 2,
        out_specs=[whole] * 3,
    )
    return call(
        finish_kernel,
        [shape] * 2,
        (odd, early_near, last_near, early_far, last_far, places),
        in_specs=[scalar] + [whole] * 5,
        out_specs=[outside] * 2,
        scratch_shapes=[pltpu.VMEM((tokens, width), BF16)] * 2 + [pltpu.SemaphoreType.DMA((2,))],
    )


def on_device(section_in_a, route_a, router, gate_up, down_proj, section_in_b, route_b, grad_out_b):
    groups = lax.axis_size("expert")
    pipe = lax.axis_size("pipe")
    me = lax.axis_index("expert")
    wsplit = min(8, groups)
    flight = groups // wsplit
    mine = me // wsplit
    tok_rows, width = section_in_a.shape[1:]
    topk = route_a.shape[2]
    slot_count = tok_rows // 8
    slots = flight * slot_count
    router_table = router[0]
    experts = router_table.shape[1]
    hidden_width = gate_up.shape[3]
    bits = [1 << k for k in reversed(range(groups.bit_length() - 1))]

    odd = lax.axis_index("pipe") % 2
    packed, twin_rows, sel_a, sel_b = call(
        functools.partial(pick_kernel, flight, slot_count, topk),
        [
            ((3, slots, width + experts), BF16),
            ((2, slots, width), BF16),
            ((slots, tok_rows), BF16),
            ((slots, tok_rows), BF16),
        ],
        (route_b[0].T, route_a[0].T, section_in_b[0], grad_out_b[0], section_in_a[0]),
        limit=61,
        in_specs=[outside] * 5,
        out_specs=[whole] * 4,
        scratch_shapes=[pltpu.VMEM((topk, tok_rows), jnp.int32)] * 2
        + [pltpu.VMEM((tok_rows, width), BF16)] * 3
        + [pltpu.SemaphoreType.DMA((5,))],
    )

    def ordered(sends_a, lanes, after):
        return call(
            functools.partial(order_kernel, flight, slots, sends_a),
            [
                ((slots, width), BF16),
                ((slots, tok_rows), BF16),
                ((tok_rows - slots, width + lanes), BF16),
            ],
            (odd.reshape(1), route_a[0].T, route_b[0].T, section_in_a[0], grad_out_b[0], *after),
            limit=61,
            in_specs=[scalar] + [outside] * 4 + [anywhere] * len(after),
            out_specs=[whole] * 3,
            scratch_shapes=[
                pltpu.VMEM((topk, tok_rows), jnp.int32),
                pltpu.VMEM((tok_rows, width), BF16),
                pltpu.SemaphoreType.DMA((2,)),
            ],
        )

    def everywhere(block):
        pieces = [block]
        for bit in bits:
            pieces += [exchanged(piece, bit) for piece in pieces]
        return pieces

    def of_mine(piece):
        if flight == 1:
            return piece
        split = piece.reshape(piece.shape[0], flight, slot_count, piece.shape[2])
        return lax.dynamic_index_in_dim(split, mine, axis=1, keepdims=False)

    def spread(values):
        if flight == 1:
            return values
        here = (jnp.arange(flight) == mine)[:, None, None]
        full = jnp.where(here, values[..., None, :, :], jnp.zeros((), values.dtype))
        return full.reshape(values.shape[:-2] + (slots, values.shape[-1]))

    own_all = everywhere(packed)
    first_near, at_near, to_near = ordered(0, tok_rows, ())
    from_near = lax.ppermute(to_near, "pipe", near(pipe))
    first_far, at_far, to_far = ordered(1, tok_rows // 2, own_all[1:2])
    from_far = lax.ppermute(to_far, "pipe", far(pipe))
    twin_all = everywhere(lax.ppermute(twin_rows, "pipe", twins(pipe)))
    twin = [of_mine(p) for p in twin_all]
    own = [of_mine(p) for p in own_all]
    rows_all = groups * slot_count
    lanes = 2 * width + 128

    *parts, basis, factors = call(
        functools.partial(expert_kernel, groups, topk),
        [((slot_count, lanes), BF16)] * groups
        + [((groups, slot_count, experts), F32), ((rows_all, 3 * hidden_width), BF16)],
        (mine.reshape(1), *own, router_table, gate_up[0], down_proj[0]),
        limit=50,
        in_specs=[scalar] + [whole] * groups + [outside] * 3,
        out_specs=[whole] * (groups + 2),
        scratch_shapes=[
            pltpu.VMEM((2 * rows_all, width), BF16),
            pltpu.VMEM((rows_all, width), BF16),
            pltpu.VMEM((2 * rows_all, experts), F32),
            pltpu.VMEM((width, experts), BF16),
            pltpu.VMEM((2, width, hidden_width), BF16),
            pltpu.VMEM((hidden_width, width), BF16),
            pltpu.SemaphoreType.DMA((4,)),
        ],
    )
    if flight > 1:
        held = jnp.concatenate([piece[0] for piece in own_all]).reshape(groups * slots, -1)
        named = jnp.tile(jnp.repeat(jnp.arange(flight), slot_count), groups)
        basis = gates(
            held[:, width:].astype(F32),
            dot(held[:, :width], router_table),
            topk,
            named.astype(F32)[:, None],
        )[1].reshape(groups, slots, experts)
    terms = [[spread(part)] for part in parts]
    span, carrier = groups, terms[0][0]
    for bit in reversed(bits):
        sums = [terms[j][0] for j in range(span // 2, span)]
        split = span == 2
        if span < groups:
            sizes = [len(terms[j]) for j in range(span // 2, span)]
            given = [term for j in range(span // 2, span) for term in terms[j]]
            sums = call(
                functools.partial(middle_kernel, groups, span, sizes, split),
                [((slots, width), BF16), ((slots, width + 128), BF16)]
                if split
                else [((slots, lanes), BF16)] * len(sizes),
                (carrier, terms[span - 1][-1], *given, *twin_all),
                in_specs=[whole] * (2 + len(given)) + [anywhere] * groups,
                out_specs=[whole] * (2 if split else len(sizes)),
            )
            carrier = sums[-1]
        span //= 2
        if split:
            terms[0] += [exchanged(value, bit) for value in sums]
        else:
            for j in reversed(range(span)):
                terms[j].append(exchanged(sums[j], bit))
    last_near, last_far, wide = call(
        functools.partial(last_kernel, groups, span, len(terms[0])),
        [
            ((slots, width), BF16),
            ((slots, width), BF16),
            ((groups, slot_count, 3 * hidden_width + flight * experts), BF16),
        ],
        (
            odd.reshape(1),
            carrier,
            *terms[0],
            basis,
            router_table,
            factors,
            sel_a,
            sel_b,
            first_near,
            first_far,
            at_near,
            at_far,
        ),
        in_specs=[scalar] + [whole] * (len(terms[0]) + 10),
        out_specs=[whole] * 3,
    )
    twin_wide = lax.ppermute(wide, "pipe", twins(pipe))
    last_near = lax.ppermute(last_near, "pipe", near(pipe))
    last_far = lax.ppermute(last_far, "pipe", far(pipe))

    share = width // groups
    tiles = min(8, share // 128)
    tile = width // tiles
    same = flight == 1
    held = (*own, *twin) if same else (*own, *twin, *own_all, *twin_all)
    grad_gate_up, grad_down, grad_router = call(
        functools.partial(grads_kernel, groups, hidden_width, experts, same),
        [
            ((2, width, hidden_width), BF16),
            ((hidden_width, width), BF16),
            ((share, experts), BF16),
        ],
        (me.reshape(1), *held, wide, twin_wide),
        grid=(tiles,),
        in_specs=[scalar] + [whole] * (len(held) + 2),
        out_specs=[
            pl.BlockSpec((2, tile, hidden_width), lambda i: (0, i, 0)),
            pl.BlockSpec((hidden_width, tile), lambda i: (0, i)),
            pl.BlockSpec((share // tiles, experts), lambda i: (i, 0)),
        ],
    )
    section_out_a, grad_in_b = placed(odd.reshape(1), last_near, from_near, last_far, from_far)
    return (
        section_out_a[None],
        grad_in_b[None],
        grad_gate_up[None],
        grad_down[None],
        grad_router[None],
    )


def solution(mesh):
    return jax.shard_map(
        on_device,
        mesh=mesh,
        in_specs=(
            P("pipe", "expert", None),
            P("pipe", "expert", None),
            P("pipe", None, None),
            P("pipe", None, None, "expert"),
            P("pipe", "expert", None),
            P("pipe", "expert", None),
            P("pipe", "expert", None),
            P("pipe", "expert", None),
        ),
        out_specs=(
            P("pipe", "expert", None),
            P("pipe", "expert", None),
            P("pipe", None, None, "expert"),
            P("pipe", "expert", None),
            P("pipe", "expert", None),
        ),
        check_vma=False,
    )
```

```python
import functools

import jax
import jax.numpy as jnp
from jax import lax
from jax.experimental import pallas as pl
from jax.experimental.pallas import tpu as pltpu
from jax.sharding import PartitionSpec as P

F32, BF16 = jnp.float32, jnp.bfloat16
whole = pl.BlockSpec(memory_space=pltpu.VMEM)
anywhere = pl.BlockSpec(memory_space=pl.ANY)
outside = pl.BlockSpec(memory_space=pltpu.HBM)
scalar = pl.BlockSpec(memory_space=pltpu.SMEM)
last_last = (((1,), (1,)), ((), ()))
first_first = (((0,), (0,)), ((), ()))
MIB = 1 << 20


def dot(a, b, dims=(((1,), (0,)), ((), ()))):
    return lax.dot_general(a, b, dims, preferred_element_type=F32)


def near(count):
    return [(i, i ^ 1) for i in range(count)]


def far(count):
    return [(i, (i + 1 if i % 2 else i - 1) % count) for i in range(count)]


def twins(count):
    return [(i, count - 1 - i) for i in range(count)]


def exchanged(block, bit):
    count = lax.axis_size("expert")
    return lax.ppermute(block, "expert", [(i, i ^ bit) for i in range(count)])


def call(kernel, outs, args, limit=24, **more):
    return pl.pallas_call(
        kernel,
        out_shape=[jax.ShapeDtypeStruct(shape, dtype) for shape, dtype in outs],
        compiler_params=pltpu.CompilerParams(vmem_limit_bytes=limit * MIB),
        cost_estimate=pl.CostEstimate(flops=0, bytes_accessed=0, transcendentals=0),
        **more,
    )(*args)


def slot_select(ids, flight, slot_count):
    tokens = ids.shape[1]
    earlier = (
        lax.broadcasted_iota(jnp.int32, (tokens, tokens), 0)
        < lax.broadcasted_iota(jnp.int32, (tokens, tokens), 1)
    ).astype(F32).astype(BF16)
    slot_ids = lax.broadcasted_iota(jnp.int32, (slot_count, tokens), 0).astype(F32)
    picked = []
    for f in range(flight):
        named = jnp.max((ids == f).astype(F32), axis=0, keepdims=True)
        named = jnp.broadcast_to(named, (slot_count, tokens))
        rank = dot(named.astype(BF16), earlier)
        picked.append(jnp.where(rank == slot_ids, named, 0.0))
    return jnp.concatenate(picked, axis=0).astype(BF16)


def token_places(ids, flight):
    tokens = ids.shape[1]
    earlier = (
        lax.broadcasted_iota(jnp.int32, (tokens, tokens), 0)
        < lax.broadcasted_iota(jnp.int32, (tokens, tokens), 1)
    ).astype(F32).astype(BF16)
    token = lax.broadcasted_iota(jnp.int32, (8, tokens), 1).astype(F32)
    named = jnp.max((ids < flight).astype(F32), axis=0, keepdims=True)
    named = jnp.broadcast_to(named, (8, tokens))
    rank = dot(named.astype(BF16), earlier)
    count = jnp.sum(named, axis=1, keepdims=True)
    return jnp.where(named > 0.0, rank, count + token - rank)[:1]


def order_of(places):
    tokens = places.shape[1]
    place = lax.broadcasted_iota(jnp.int32, (tokens, tokens), 0).astype(F32)
    return (place == places).astype(F32).astype(BF16)


def pick_kernel(flight, slot_count, topk, odd, *refs):
    sources, refs = refs[:5], refs[5:]
    packed, twin, sel_a, sel_b, first_near, first_far, at_near, at_far, to_near, to_far = refs[:10]
    held, blocks, sems = refs[10:15], refs[15:17], refs[17]
    copies = [
        pltpu.make_async_copy(source, here, sems.at[k])
        for k, (source, here) in enumerate(zip(sources, held))
    ]
    onward = [
        pltpu.make_async_copy(block, out, sems.at[5 + k])
        for k, (block, out) in enumerate(zip(blocks, (to_near, to_far)))
    ]
    ids_b, ids_a, x_b, grad, x_a = held
    tokens, width = x_b.shape
    slots = first_near.shape[0]
    lanes = packed.shape[2] - width

    def send(k, ids_ref, block_ref):
        first, at, block = ((first_near, at_near), (first_far, at_far))[k] + (blocks[k],)
        places = token_places(ids_ref[...], flight)
        at[...] = jnp.broadcast_to(places, at.shape).astype(BF16)
        rows = dot(order_of(places), block_ref[...]).astype(BF16)
        first[...] = rows[:slots]
        block[:, :width] = rows[slots:]
        if block.shape[1] > width:
            block[:, width:] = jnp.broadcast_to(places, (tokens - slots, tokens)).astype(BF16)
        onward[k].start()

    def pick(ids_ref, select_ref, wanted):
        ids = ids_ref[...]
        select = slot_select(ids, flight, slot_count)
        select_ref[...] = select
        spare = jnp.zeros((lanes - topk, tokens), F32)
        numbers = jnp.concatenate([ids.astype(F32), spare], axis=0).astype(BF16)
        slot_ids = dot(select, numbers, last_last).astype(BF16)
        for place, source in wanted:
            rows = dot(select, held[source][...]).astype(BF16)
            packed[place, :, :width] = rows
            packed[place, :, width:] = slot_ids
            if place < 2:
                twin[place] = rows

    for mine, near, far in ((0, (1, 4), (0, 3)), (1, (0, 3), (1, 4))):

        @pl.when(odd[0] == mine)
        def _(near=near, far=far):
            for k in (*near, *far, 2):
                copies[k].start()
            for k in near:
                copies[k].wait()
            send(0, *(held[k] for k in near))
            for k in far:
                copies[k].wait()
            send(1, *(held[k] for k in far))

    copies[2].wait()
    pick(ids_b, sel_b, ((0, 2), (1, 3)))
    pick(ids_a, sel_a, ((2, 4),))
    for copy in onward:
        copy.wait()


def gates(ids, logits, topk, expert):
    lanes = lax.broadcasted_iota(jnp.int32, logits.shape, 1).astype(F32)
    picks = [ids[:, k : k + 1] for k in range(topk)]
    chosen = [
        jnp.sum(jnp.where(lanes == pick, logits, 0.0), axis=1, keepdims=True) for pick in picks
    ]
    top = functools.reduce(jnp.maximum, chosen)
    powers = [jnp.exp(value - top) for value in chosen]
    scale = 1.0 / functools.reduce(jnp.add, powers)
    probs = [power * scale for power in powers]
    named = [(pick == expert).astype(F32) for pick in picks]
    weight = functools.reduce(jnp.add, [p * n for p, n in zip(probs, named)])
    basis = functools.reduce(
        jnp.add,
        [jnp.where(lanes == pick, p * (n - weight), 0.0) for pick, p, n in zip(picks, probs, named)],
    )
    return weight, basis


def coded(columns, lanes):
    rows = columns[0].shape[0]
    lane = lax.broadcasted_iota(jnp.int32, (rows, lanes), 1)
    out = jnp.zeros((rows, lanes), F32)
    for j, rest in enumerate(columns):
        for k in range(3):
            term = rest.astype(BF16).astype(F32)
            out = jnp.where(lane == 3 * j + k, term, out)
            rest = rest - term
    return out.astype(BF16)


def decoded(code, count):
    code = code.astype(F32)
    return [
        code[:, 3 * j : 3 * j + 1] + code[:, 3 * j + 1 : 3 * j + 2] + code[:, 3 * j + 2 : 3 * j + 3]
        for j in range(count)
    ]


def summed_scores(own, other, blocks, span, width):
    mine, theirs = decoded(own[:, width:], blocks), decoded(other[:, width:], blocks)
    return [mine[j] + theirs[j ^ span] for j in range(blocks)]


def expert_kernel(blocks, topk, mine, *refs):
    pieces, refs = refs[:blocks], refs[blocks:]
    sources, refs = refs[:3], refs[3:]
    parts, refs = refs[:blocks], refs[blocks:]
    basis_out, factors, rows, grads, ids, router, gate_up, down, sems = refs
    copies = [
        pltpu.make_async_copy(source, here, sems.at[k])
        for k, (source, here) in enumerate(
            (
                (sources[1].at[0], gate_up.at[0]),
                (sources[1].at[1], gate_up.at[1]),
                (sources[2], down),
                (sources[0], router),
            )
        )
    ]
    for copy in copies:
        copy.start()
    slot_count = pieces[0].shape[1]
    width, hidden_width = gate_up.shape[1], gate_up.shape[2]
    half = blocks * slot_count
    for place in range(blocks):
        piece = pieces[place]
        here = pl.ds(place * slot_count, slot_count)
        there = pl.ds(half + place * slot_count, slot_count)
        rows[here, :] = piece[0, :, :width]
        rows[there, :] = piece[2, :, :width]
        grads[here, :] = piece[1, :, :width]
        ids[here, :] = piece[0, :, width:].astype(F32)
        ids[there, :] = piece[2, :, width:].astype(F32)
    copies[0].wait()
    act_gate = dot(rows[...], gate_up[0])
    copies[1].wait()
    act_up = dot(rows[...], gate_up[1])
    copies[2].wait()
    back = dot(grads[...], down[...], last_last)
    copies[3].wait()
    weight, basis = gates(ids[...], dot(rows[...], router[...]), topk, mine[0].astype(F32))
    logistic = jax.nn.sigmoid(act_gate)
    hidden = act_gate * logistic * act_up
    weight_b = weight[:half]
    hidden_b, gate_b, up_b, log_b = hidden[:half], act_gate[:half], act_up[:half], logistic[:half]
    basis_out[...] = basis[:half].reshape(basis_out.shape)
    scores = jnp.sum(hidden_b * back, axis=1, keepdims=True)
    code = coded(
        [scores[j * slot_count : (j + 1) * slot_count] for j in range(blocks)],
        parts[0].shape[1] - 2 * width,
    )
    d_hidden = weight_b * back
    d_gate = (d_hidden * up_b * log_b * (1.0 + gate_b * (1.0 - log_b))).astype(BF16)
    d_up = (d_hidden * gate_b * log_b).astype(BF16)
    factors[:, :hidden_width] = d_gate
    factors[:, hidden_width : 2 * hidden_width] = d_up
    factors[:, 2 * hidden_width :] = (weight_b * hidden_b).astype(BF16)
    hidden_a = (weight[half:] * hidden[half:]).astype(BF16)
    step = min(width, 512)
    for first in range(0, width, step):
        cols = slice(first, first + step)
        part_a = dot(hidden_a, down[:, cols]).astype(BF16)
        part_b = (
            dot(d_gate, gate_up[0, cols, :], last_last) + dot(d_up, gate_up[1, cols, :], last_last)
        ).astype(BF16)
        for j, part in enumerate(parts):
            here = slice(j * slot_count, (j + 1) * slot_count)
            part[:, cols] = part_a[here]
            part[:, first + width : first + width + step] = part_b[here]
    for part in parts:
        part[:, 2 * width :] = code


def added(terms, width):
    return functools.reduce(jnp.add, [term[:, :width].astype(F32) for term in terms])


def middle_kernel(blocks, span, sizes, split, own, other, *refs):
    terms, outs = refs[: sum(sizes)], refs[sum(sizes) + blocks :]
    lanes = own.shape[1] - 128
    code = coded(summed_scores(own, other, blocks, span, lanes), 128)
    for size in sizes:
        total = added(terms[:size], lanes).astype(BF16)
        if split:
            outs[0][...] = total[:, : lanes // 2]
            outs[1][:, : lanes // 2] = total[:, lanes // 2 :]
            outs[1][:, lanes // 2 :] = code
        else:
            outs[0][:, :lanes] = total
            outs[0][:, lanes:] = code
            outs = outs[1:]
        terms = terms[size:]


def last_kernel(blocks, span, count, odd, own, *refs):
    terms, refs = refs[: count - 2], refs[count - 2 :]
    last_a, last_b, basis, router, factors, sel_a, sel_b = refs[:7]
    first_near, first_far, at_near, at_far, to_near, to_far, wide = refs[7:]
    width, experts = router.shape
    slots = first_near.shape[0]
    total = added(terms, 2 * width)
    scores = summed_scores(own, last_b, blocks, span, width)
    sums = [(score * basis[j]).astype(BF16) for j, score in enumerate(scores)]
    more_a = total[:, :width] + last_a[...].astype(F32)
    more_b = (
        total[:, width:] + last_b[:, :width].astype(F32) + dot(sums[0], router[...], last_last)
    )
    even = odd[0] == 0
    for sends_a, first, at, out in (
        (even, first_near, at_near, to_near),
        (jnp.logical_not(even), first_far, at_far, to_far),
    ):
        more = jnp.where(sends_a, more_a, more_b)
        if slots * blocks != factors.shape[0]:
            places = at[...].astype(F32)
            row = (lax.broadcasted_iota(jnp.int32, places.shape, 0).astype(F32) == places)
            row = row.astype(F32).astype(BF16)
            slot = jnp.where(sends_a, sel_a[...].astype(F32), sel_b[...].astype(F32)).astype(BF16)
            more = jnp.dot(dot(row, slot, last_last), more, precision=lax.Precision.HIGHEST)
        out[:, :width] = (first[...].astype(F32) + more).astype(BF16)
        if out.shape[1] > width:
            out[:, width:] = at[...]
    slot_count = factors.shape[0] // blocks
    core = factors.shape[1]
    for j, value in enumerate(sums):
        wide[j, :, :core] = factors[j * slot_count : (j + 1) * slot_count, :]
        for f in range(value.shape[0] // slot_count):
            wide[j, :, core + f * experts : core + (f + 1) * experts] = value[
                f * slot_count : (f + 1) * slot_count
            ]


def grads_kernel(blocks, hidden_width, experts, same, me, *refs):
    pieces, refs = refs[: 2 * blocks], refs[2 * blocks :]
    pieces_all = pieces
    if not same:
        pieces_all, refs = refs[: 2 * blocks], refs[2 * blocks :]
    own_wide, twin_wide, gate_up, down, router, mark = refs
    mark[...] = jnp.zeros_like(mark)
    i = pl.program_id(0)
    tile, share_tile = down.shape[1], router.shape[0]
    share = share_tile * pl.num_programs(0)
    cols = pl.ds(pl.multiple_of(i * tile, tile), tile)
    mine = pl.ds(pl.multiple_of(me[0] * share + i * share_tile, 128), share_tile)

    def stacked(held, which, where):
        return jnp.concatenate([piece[which, :, where] for piece in held])

    def column(first, size):
        return jnp.concatenate(
            [w[j, :, first : first + size] for w in (own_wide, twin_wide) for j in range(blocks)]
        )

    core = 3 * hidden_width
    both = dot(stacked(pieces, 0, cols), column(0, 2 * hidden_width), first_first).astype(BF16)
    gate_up[0] = both[:, :hidden_width]
    gate_up[1] = both[:, hidden_width:]
    down[...] = dot(
        column(2 * hidden_width, hidden_width), stacked(pieces, 1, cols), first_first
    ).astype(BF16)
    flight = (own_wide.shape[2] - core) // experts
    lg = jnp.concatenate(
        [
            w[j, :, core + f * experts : core + (f + 1) * experts]
            for w in (own_wide, twin_wide)
            for j in range(blocks)
            for f in range(flight)
        ]
    )
    router[...] = dot(stacked(pieces_all, 0, mine), lg, first_first).astype(BF16)


def pass_kernel(*refs):
    pass


def place_kernel(to_a, odd, block, last, _, out_a, out_b, mark, held, sem):
    tokens, width = held.shape
    step = width // 4
    order = order_of(last[:1, width:].astype(F32))
    for c in range(4):
        cols = slice(c * step, (c + 1) * step)
        rows = jnp.concatenate([last[:, cols], block[:, cols]])
        held[:, cols] = dot(order, rows, first_first).astype(BF16)
        for mine, out in ((to_a, out_a), (1 - to_a, out_b)):

            @pl.when(odd[0] == mine)
            def _(out=out, cols=cols):
                pltpu.make_async_copy(held.at[:, cols], out.at[:, cols], sem).start()

    mark[...] = jnp.zeros_like(mark)
    pltpu.make_async_copy(held, out_a, sem).wait()


def placed(to_a, odd, block, last, after):
    width = block.shape[1]
    tokens = block.shape[0] + last.shape[0]
    return call(
        functools.partial(place_kernel, to_a),
        [((tokens, width), BF16)] * 2 + [((8, 128), F32)],
        (odd, block, last, after),
        in_specs=[scalar] + [whole] * 3,
        out_specs=[outside] * 2 + [whole],
        scratch_shapes=[pltpu.VMEM((tokens, width), BF16), pltpu.SemaphoreType.DMA],
    )


def early_kernel(block, _, out, places):
    tokens, width = out.shape
    step = width // 4
    places[...] = jnp.broadcast_to(block[:1, width:].astype(F32), places.shape)
    order = order_of(places[:1, :])[tokens - block.shape[0] :]
    for c in range(4):
        cols = slice(c * step, (c + 1) * step)
        out[:, cols] = dot(order, block[:, cols], first_first).astype(BF16)


def finish_kernel(to_a, odd, early, places, last, *refs):
    outs, held, sem = refs[-4:-2], refs[-2], refs[-1]
    tokens, width = held.shape
    step = width // 4
    order = order_of(places[:1, :])[: last.shape[0]]
    for c in range(4):
        cols = slice(c * step, (c + 1) * step)
        late = dot(order, last[:, cols], first_first).astype(BF16)
        held[:, cols] = early[:, cols] + late
        for mine, out in ((to_a, outs[0]), (1 - to_a, outs[1])):

            @pl.when(odd[0] == mine)
            def _(out=out, cols=cols):
                pltpu.make_async_copy(held.at[:, cols], out.at[:, cols], sem).start()

    pltpu.make_async_copy(held, outs[0], sem).wait()


def placed_in_two(to_a, odd, block, last, before, after):
    slots, width = last.shape
    tokens = block.shape[0] + slots
    early, places = call(
        early_kernel,
        [((tokens, width), BF16), ((8, tokens), F32)],
        (block, after),
        in_specs=[whole] * 2,
        out_specs=[whole] * 2,
    )
    return call(
        functools.partial(finish_kernel, to_a),
        [((tokens, width), BF16)] * 2,
        (odd, early, places, last, *before),
        in_specs=[scalar] + [whole] * 3 + [outside] * 2,
        out_specs=[outside] * 2,
        scratch_shapes=[pltpu.VMEM((tokens, width), BF16), pltpu.SemaphoreType.DMA],
        input_output_aliases={4: 0, 5: 1},
    )


def on_device(section_in_a, route_a, router, gate_up, down_proj, section_in_b, route_b, grad_out_b):
    groups = lax.axis_size("expert")
    pipe = lax.axis_size("pipe")
    me = lax.axis_index("expert")
    wsplit = min(8, groups)
    flight = groups // wsplit
    mine = me // wsplit
    tok_rows, width = section_in_a.shape[1:]
    topk = route_a.shape[2]
    slot_count = tok_rows // 8
    slots = flight * slot_count
    router_table = router[0]
    experts = router_table.shape[1]
    hidden_width = gate_up.shape[3]
    bits = [1 << k for k in reversed(range(groups.bit_length() - 1))]

    odd = lax.axis_index("pipe") % 2
    sources = (route_b[0].T, route_a[0].T, section_in_b[0], grad_out_b[0], section_in_a[0])
    packed, twin_rows, sel_a, sel_b, first_near, first_far, at_near, at_far, to_near, to_far = call(
        functools.partial(pick_kernel, flight, slot_count, topk),
        [
            ((3, slots, width + experts), BF16),
            ((2, slots, width), BF16),
            ((slots, tok_rows), BF16),
            ((slots, tok_rows), BF16),
            ((slots, width), BF16),
            ((slots, width), BF16),
            ((slots, tok_rows), BF16),
            ((slots, tok_rows), BF16),
            ((tok_rows - slots, width + tok_rows), BF16),
            ((tok_rows - slots, width), BF16),
        ],
        (odd.reshape(1), *sources),
        limit=61,
        in_specs=[scalar] + [outside] * 5,
        out_specs=[whole] * 8 + [outside] * 2,
        scratch_shapes=[pltpu.VMEM((topk, tok_rows), jnp.int32)] * 2
        + [pltpu.VMEM((tok_rows, width), BF16)] * 3
        + [
            pltpu.VMEM((tok_rows - slots, width + tok_rows), BF16),
            pltpu.VMEM((tok_rows - slots, width), BF16),
        ]
        + [pltpu.SemaphoreType.DMA((7,))],
    )

    def everywhere(block):
        pieces = [block]
        for bit in bits:
            pieces += [exchanged(piece, bit) for piece in pieces]
        return pieces

    def of_mine(piece):
        if flight == 1:
            return piece
        split = piece.reshape(piece.shape[0], flight, slot_count, piece.shape[2])
        return lax.dynamic_index_in_dim(split, mine, axis=1, keepdims=False)

    def spread(values):
        if flight == 1:
            return values
        here = (jnp.arange(flight) == mine)[:, None, None]
        full = jnp.where(here, values[..., None, :, :], jnp.zeros((), values.dtype))
        return full.reshape(values.shape[:-2] + (slots, values.shape[-1]))

    own_all = everywhere(packed)
    from_near = lax.ppermute(to_near, "pipe", near(pipe))
    from_twin = lax.ppermute(twin_rows, "pipe", twins(pipe))
    (to_far,) = call(
        pass_kernel,
        [(to_far.shape, BF16)],
        (to_far, from_twin),
        in_specs=[outside, anywhere],
        out_specs=[outside],
        input_output_aliases={0: 0},
    )
    from_far = lax.ppermute(to_far, "pipe", far(pipe))
    twin_all = everywhere(from_twin)
    twin = [of_mine(p) for p in twin_all]
    own = [of_mine(p) for p in own_all]
    rows_all = groups * slot_count
    lanes = 2 * width + 128

    *parts, basis, factors = call(
        functools.partial(expert_kernel, groups, topk),
        [((slot_count, lanes), BF16)] * groups
        + [((groups, slot_count, experts), F32), ((rows_all, 3 * hidden_width), BF16)],
        (mine.reshape(1), *own, router_table, gate_up[0], down_proj[0]),
        limit=50,
        in_specs=[scalar] + [whole] * groups + [outside] * 3,
        out_specs=[whole] * (groups + 2),
        scratch_shapes=[
            pltpu.VMEM((2 * rows_all, width), BF16),
            pltpu.VMEM((rows_all, width), BF16),
            pltpu.VMEM((2 * rows_all, experts), F32),
            pltpu.VMEM((width, experts), BF16),
            pltpu.VMEM((2, width, hidden_width), BF16),
            pltpu.VMEM((hidden_width, width), BF16),
            pltpu.SemaphoreType.DMA((4,)),
        ],
    )
    if flight > 1:
        held = jnp.concatenate([piece[0] for piece in own_all]).reshape(groups * slots, -1)
        named = jnp.tile(jnp.repeat(jnp.arange(flight), slot_count), groups)
        basis = gates(
            held[:, width:].astype(F32),
            dot(held[:, :width], router_table),
            topk,
            named.astype(F32)[:, None],
        )[1].reshape(groups, slots, experts)
    terms = [[spread(part)] for part in parts]
    span, carrier = groups, terms[0][0]
    for bit in reversed(bits):
        sums = [terms[j][0] for j in range(span // 2, span)]
        split = span == 2
        if span < groups:
            sizes = [len(terms[j]) for j in range(span // 2, span)]
            given = [term for j in range(span // 2, span) for term in terms[j]]
            sums = call(
                functools.partial(middle_kernel, groups, span, sizes, split),
                [((slots, width), BF16), ((slots, width + 128), BF16)]
                if split
                else [((slots, lanes), BF16)] * len(sizes),
                (carrier, terms[span - 1][-1], *given, *twin_all),
                in_specs=[whole] * (2 + len(given)) + [anywhere] * groups,
                out_specs=[whole] * (2 if split else len(sizes)),
            )
            carrier = sums[-1]
        span //= 2
        if split:
            terms[0] += [exchanged(value, bit) for value in sums]
        else:
            for j in reversed(range(span)):
                terms[j].append(exchanged(sums[j], bit))
    last_near, last_far, wide = call(
        functools.partial(last_kernel, groups, span, len(terms[0])),
        [
            ((slots, width), BF16),
            ((slots, width + tok_rows), BF16),
            ((groups, slot_count, 3 * hidden_width + flight * experts), BF16),
        ],
        (
            odd.reshape(1),
            carrier,
            *terms[0],
            basis,
            router_table,
            factors,
            sel_a,
            sel_b,
            first_near,
            first_far,
            at_near,
            at_far,
        ),
        in_specs=[scalar] + [whole] * (len(terms[0]) + 10),
        out_specs=[whole] * 3,
    )
    twin_wide = lax.ppermute(wide, "pipe", twins(pipe))
    last_near = lax.ppermute(last_near, "pipe", near(pipe))
    last_far = lax.ppermute(last_far, "pipe", far(pipe))

    share = width // groups
    tiles = min(8, share // 128)
    tile = width // tiles
    same = flight == 1
    held = (*own, *twin) if same else (*own, *twin, *own_all, *twin_all)
    grad_gate_up, grad_down, grad_router, mark = call(
        functools.partial(grads_kernel, groups, hidden_width, experts, same),
        [
            ((2, width, hidden_width), BF16),
            ((hidden_width, width), BF16),
            ((share, experts), BF16),
            ((8, 128), F32),
        ],
        (me.reshape(1), *held, wide, twin_wide),
        grid=(tiles,),
        in_specs=[scalar] + [whole] * (len(held) + 2),
        out_specs=[
            pl.BlockSpec((2, tile, hidden_width), lambda i: (0, i, 0)),
            pl.BlockSpec((hidden_width, tile), lambda i: (0, i)),
            pl.BlockSpec((share // tiles, experts), lambda i: (i, 0)),
            pl.BlockSpec((8, 128), lambda i: (0, 0)),
        ],
    )
    odd = odd.reshape(1)
    *outs, mark = placed(0, odd, from_far, last_far, mark)
    section_out_a, grad_in_b = placed_in_two(1, odd, from_near, last_near, outs, mark)
    return (
        section_out_a[None],
        grad_in_b[None],
        grad_gate_up[None],
        grad_down[None],
        grad_router[None],
    )


def solution(mesh):
    return jax.shard_map(
        on_device,
        mesh=mesh,
        in_specs=(
            P("pipe", "expert", None),
            P("pipe", "expert", None),
            P("pipe", None, None),
            P("pipe", None, None, "expert"),
            P("pipe", "expert", None),
            P("pipe", "expert", None),
            P("pipe", "expert", None),
            P("pipe", "expert", None),
        ),
        out_specs=(
            P("pipe", "expert", None),
            P("pipe", "expert", None),
            P("pipe", None, None, "expert"),
            P("pipe", "expert", None),
            P("pipe", "expert", None),
        ),
        check_vma=False,
    )
```

```python
import functools

import jax
import jax.numpy as jnp
from jax import lax
from jax.experimental import pallas as pl
from jax.experimental.pallas import tpu as pltpu
from jax.sharding import PartitionSpec as P

F32, BF16 = jnp.float32, jnp.bfloat16
whole = pl.BlockSpec(memory_space=pltpu.VMEM)
anywhere = pl.BlockSpec(memory_space=pl.ANY)
outside = pl.BlockSpec(memory_space=pltpu.HBM)
scalar = pl.BlockSpec(memory_space=pltpu.SMEM)
last_last = (((1,), (1,)), ((), ()))
first_first = (((0,), (0,)), ((), ()))
MIB = 1 << 20


def dot(a, b, dims=(((1,), (0,)), ((), ()))):
    return lax.dot_general(a, b, dims, preferred_element_type=F32)


def near(count):
    return [(i, i ^ 1) for i in range(count)]


def far(count):
    return [(i, (i + 1 if i % 2 else i - 1) % count) for i in range(count)]


def twins(count):
    return [(i, count - 1 - i) for i in range(count)]


def exchanged(block, bit):
    count = lax.axis_size("expert")
    return lax.ppermute(block, "expert", [(i, i ^ bit) for i in range(count)])


def call(kernel, outs, args, limit=24, **more):
    return pl.pallas_call(
        kernel,
        out_shape=[jax.ShapeDtypeStruct(shape, dtype) for shape, dtype in outs],
        compiler_params=pltpu.CompilerParams(vmem_limit_bytes=limit * MIB),
        cost_estimate=pl.CostEstimate(flops=0, bytes_accessed=0, transcendentals=0),
        **more,
    )(*args)


def slot_select(ids, flight, slot_count):
    tokens = ids.shape[1]
    earlier = (
        lax.broadcasted_iota(jnp.int32, (tokens, tokens), 0)
        < lax.broadcasted_iota(jnp.int32, (tokens, tokens), 1)
    ).astype(F32).astype(BF16)
    slot_ids = lax.broadcasted_iota(jnp.int32, (slot_count, tokens), 0).astype(F32)
    picked = []
    for f in range(flight):
        named = jnp.max((ids == f).astype(F32), axis=0, keepdims=True)
        named = jnp.broadcast_to(named, (slot_count, tokens))
        rank = dot(named.astype(BF16), earlier)
        picked.append(jnp.where(rank == slot_ids, named, 0.0))
    return jnp.concatenate(picked, axis=0).astype(BF16)


def token_places(ids, flight):
    tokens = ids.shape[1]
    earlier = (
        lax.broadcasted_iota(jnp.int32, (tokens, tokens), 0)
        < lax.broadcasted_iota(jnp.int32, (tokens, tokens), 1)
    ).astype(F32).astype(BF16)
    token = lax.broadcasted_iota(jnp.int32, (8, tokens), 1).astype(F32)
    named = jnp.max((ids < flight).astype(F32), axis=0, keepdims=True)
    named = jnp.broadcast_to(named, (8, tokens))
    rank = dot(named.astype(BF16), earlier)
    count = jnp.sum(named, axis=1, keepdims=True)
    return jnp.where(named > 0.0, rank, count + token - rank)[:1]


def order_of(places):
    tokens = places.shape[1]
    place = lax.broadcasted_iota(jnp.int32, (tokens, tokens), 0).astype(F32)
    return (place == places).astype(F32).astype(BF16)


def pick_kernel(flight, slot_count, topk, odd, *refs):
    sources, refs = refs[:5], refs[5:]
    packed, twin, sel_a, sel_b, first_near, first_far, at_near, at_far, to_near, to_far = refs[:10]
    held, blocks, sems = refs[10:15], refs[15:17], refs[17]
    copies = [
        pltpu.make_async_copy(source, here, sems.at[k])
        for k, (source, here) in enumerate(zip(sources, held))
    ]
    onward = [
        pltpu.make_async_copy(block, out, sems.at[5 + k])
        for k, (block, out) in enumerate(zip(blocks, (to_near, to_far)))
    ]
    ids_b, ids_a, x_b, grad, x_a = held
    tokens, width = x_b.shape
    slots = first_near.shape[0]
    lanes = packed.shape[2] - width

    def send(k, ids_ref, block_ref):
        first, at, block = ((first_near, at_near), (first_far, at_far))[k] + (blocks[k],)
        places = token_places(ids_ref[...], flight)
        at[...] = jnp.broadcast_to(places, at.shape).astype(BF16)
        rows = dot(order_of(places), block_ref[...]).astype(BF16)
        first[...] = rows[:slots]
        block[:, :width] = rows[slots:]
        if block.shape[1] > width:
            block[:, width:] = jnp.broadcast_to(places, (tokens - slots, tokens)).astype(BF16)
        onward[k].start()

    def pick(ids_ref, select_ref, wanted):
        ids = ids_ref[...]
        select = slot_select(ids, flight, slot_count)
        select_ref[...] = select
        spare = jnp.zeros((lanes - topk, tokens), F32)
        numbers = jnp.concatenate([ids.astype(F32), spare], axis=0).astype(BF16)
        slot_ids = dot(select, numbers, last_last).astype(BF16)
        for place, source in wanted:
            rows = dot(select, held[source][...]).astype(BF16)
            packed[place, :, :width] = rows
            packed[place, :, width:] = slot_ids
            if place < 2:
                twin[place] = rows

    for mine, near, far in ((0, (1, 4), (0, 3)), (1, (0, 3), (1, 4))):

        @pl.when(odd[0] == mine)
        def _(near=near, far=far):
            for k in (*near, *far, 2):
                copies[k].start()
            for k in near:
                copies[k].wait()
            send(0, *(held[k] for k in near))
            for k in far:
                copies[k].wait()
            send(1, *(held[k] for k in far))

    copies[2].wait()
    pick(ids_b, sel_b, ((0, 2), (1, 3)))
    pick(ids_a, sel_a, ((2, 4),))
    for copy in onward:
        copy.wait()


def gates(ids, logits, topk, expert):
    lanes = lax.broadcasted_iota(jnp.int32, logits.shape, 1).astype(F32)
    picks = [ids[:, k : k + 1] for k in range(topk)]
    chosen = [
        jnp.sum(jnp.where(lanes == pick, logits, 0.0), axis=1, keepdims=True) for pick in picks
    ]
    top = functools.reduce(jnp.maximum, chosen)
    powers = [jnp.exp(value - top) for value in chosen]
    scale = 1.0 / functools.reduce(jnp.add, powers)
    probs = [power * scale for power in powers]
    named = [(pick == expert).astype(F32) for pick in picks]
    weight = functools.reduce(jnp.add, [p * n for p, n in zip(probs, named)])
    basis = functools.reduce(
        jnp.add,
        [jnp.where(lanes == pick, p * (n - weight), 0.0) for pick, p, n in zip(picks, probs, named)],
    )
    return weight, basis


def coded(columns, lanes):
    rows = columns[0].shape[0]
    lane = lax.broadcasted_iota(jnp.int32, (rows, lanes), 1)
    out = jnp.zeros((rows, lanes), F32)
    for j, rest in enumerate(columns):
        for k in range(3):
            term = rest.astype(BF16).astype(F32)
            out = jnp.where(lane == 3 * j + k, term, out)
            rest = rest - term
    return out.astype(BF16)


def decoded(code, count):
    code = code.astype(F32)
    return [
        code[:, 3 * j : 3 * j + 1] + code[:, 3 * j + 1 : 3 * j + 2] + code[:, 3 * j + 2 : 3 * j + 3]
        for j in range(count)
    ]


def summed_scores(own, other, blocks, span, width):
    mine, theirs = decoded(own[:, width:], blocks), decoded(other[:, width:], blocks)
    return [mine[j] + theirs[j ^ span] for j in range(blocks)]


def expert_kernel(blocks, topk, mine, *refs):
    pieces, refs = refs[:blocks], refs[blocks:]
    sources, refs = refs[:3], refs[3:]
    parts, refs = refs[:blocks], refs[blocks:]
    basis_out, factors, rows, grads, ids, router, gate_up, down, sems = refs
    copies = [
        pltpu.make_async_copy(source, here, sems.at[k])
        for k, (source, here) in enumerate(
            (
                (sources[1].at[0], gate_up.at[0]),
                (sources[1].at[1], gate_up.at[1]),
                (sources[2], down),
                (sources[0], router),
            )
        )
    ]
    for copy in copies:
        copy.start()
    slot_count = pieces[0].shape[1]
    width, hidden_width = gate_up.shape[1], gate_up.shape[2]
    half = blocks * slot_count
    for place in range(blocks):
        piece = pieces[place]
        here = pl.ds(place * slot_count, slot_count)
        there = pl.ds(half + place * slot_count, slot_count)
        rows[here, :] = piece[0, :, :width]
        rows[there, :] = piece[2, :, :width]
        grads[here, :] = piece[1, :, :width]
        ids[here, :] = piece[0, :, width:].astype(F32)
        ids[there, :] = piece[2, :, width:].astype(F32)
    copies[0].wait()
    act_gate = dot(rows[...], gate_up[0])
    copies[1].wait()
    act_up = dot(rows[...], gate_up[1])
    copies[2].wait()
    back = dot(grads[...], down[...], last_last)
    copies[3].wait()
    weight, basis = gates(ids[...], dot(rows[...], router[...]), topk, mine[0].astype(F32))
    logistic = jax.nn.sigmoid(act_gate)
    hidden = act_gate * logistic * act_up
    weight_b = weight[:half]
    hidden_b, gate_b, up_b, log_b = hidden[:half], act_gate[:half], act_up[:half], logistic[:half]
    basis_out[...] = basis[:half].reshape(basis_out.shape)
    scores = jnp.sum(hidden_b * back, axis=1, keepdims=True)
    code = coded(
        [scores[j * slot_count : (j + 1) * slot_count] for j in range(blocks)],
        parts[0].shape[1] - 2 * width,
    )
    d_hidden = weight_b * back
    d_gate = (d_hidden * up_b * log_b * (1.0 + gate_b * (1.0 - log_b))).astype(BF16)
    d_up = (d_hidden * gate_b * log_b).astype(BF16)
    factors[:, :hidden_width] = d_gate
    factors[:, hidden_width : 2 * hidden_width] = d_up
    factors[:, 2 * hidden_width :] = (weight_b * hidden_b).astype(BF16)
    hidden_a = (weight[half:] * hidden[half:]).astype(BF16)
    step = min(width, 512)
    for first in range(0, width, step):
        cols = slice(first, first + step)
        part_a = dot(hidden_a, down[:, cols]).astype(BF16)
        part_b = (
            dot(d_gate, gate_up[0, cols, :], last_last) + dot(d_up, gate_up[1, cols, :], last_last)
        ).astype(BF16)
        for j, part in enumerate(parts):
            here = slice(j * slot_count, (j + 1) * slot_count)
            part[:, cols] = part_a[here]
            part[:, first + width : first + width + step] = part_b[here]
    for part in parts:
        part[:, 2 * width :] = code


def added(terms, width):
    return functools.reduce(jnp.add, [term[:, :width].astype(F32) for term in terms])


def middle_kernel(blocks, span, sizes, split, own, other, *refs):
    terms, outs = refs[: sum(sizes)], refs[sum(sizes) + blocks :]
    lanes = own.shape[1] - 128
    code = coded(summed_scores(own, other, blocks, span, lanes), 128)
    for size in sizes:
        total = added(terms[:size], lanes).astype(BF16)
        if split:
            outs[0][...] = total[:, : lanes // 2]
            outs[1][:, : lanes // 2] = total[:, lanes // 2 :]
            outs[1][:, lanes // 2 :] = code
        else:
            outs[0][:, :lanes] = total
            outs[0][:, lanes:] = code
            outs = outs[1:]
        terms = terms[size:]


def last_kernel(blocks, span, count, odd, own, *refs):
    terms, refs = refs[: count - 2], refs[count - 2 :]
    last_a, last_b, basis, router, factors, sel_a, sel_b = refs[:7]
    first_near, first_far, at_near, at_far, to_near, to_far, wide = refs[7:]
    width, experts = router.shape
    slots = first_near.shape[0]
    total = added(terms, 2 * width)
    scores = summed_scores(own, last_b, blocks, span, width)
    sums = [(score * basis[j]).astype(BF16) for j, score in enumerate(scores)]
    more_a = total[:, :width] + last_a[...].astype(F32)
    more_b = (
        total[:, width:] + last_b[:, :width].astype(F32) + dot(sums[0], router[...], last_last)
    )
    even = odd[0] == 0
    for sends_a, first, at, out in (
        (even, first_near, at_near, to_near),
        (jnp.logical_not(even), first_far, at_far, to_far),
    ):
        more = jnp.where(sends_a, more_a, more_b)
        if slots * blocks != factors.shape[0]:
            places = at[...].astype(F32)
            row = (lax.broadcasted_iota(jnp.int32, places.shape, 0).astype(F32) == places)
            row = row.astype(F32).astype(BF16)
            slot = jnp.where(sends_a, sel_a[...].astype(F32), sel_b[...].astype(F32)).astype(BF16)
            more = jnp.dot(dot(row, slot, last_last), more, precision=lax.Precision.HIGHEST)
        out[:, :width] = (first[...].astype(F32) + more).astype(BF16)
        if out.shape[1] > width:
            out[:, width:] = at[...]
    slot_count = factors.shape[0] // blocks
    core = factors.shape[1]
    for j, value in enumerate(sums):
        wide[j, :, :core] = factors[j * slot_count : (j + 1) * slot_count, :]
        for f in range(value.shape[0] // slot_count):
            wide[j, :, core + f * experts : core + (f + 1) * experts] = value[
                f * slot_count : (f + 1) * slot_count
            ]


def grads_kernel(blocks, hidden_width, experts, same, me, *refs):
    pieces, refs = refs[: 2 * blocks], refs[2 * blocks :]
    pieces_all = pieces
    if not same:
        pieces_all, refs = refs[: 2 * blocks], refs[2 * blocks :]
    own_wide, twin_wide, gate_up, down, router, mark = refs
    mark[...] = jnp.zeros_like(mark)
    i = pl.program_id(0)
    tile, share_tile = down.shape[1], router.shape[0]
    share = share_tile * pl.num_programs(0)
    cols = pl.ds(pl.multiple_of(i * tile, tile), tile)
    mine = pl.ds(pl.multiple_of(me[0] * share + i * share_tile, 128), share_tile)

    def stacked(held, which, where):
        return jnp.concatenate([piece[which, :, where] for piece in held])

    def column(first, size):
        return jnp.concatenate(
            [w[j, :, first : first + size] for w in (own_wide, twin_wide) for j in range(blocks)]
        )

    core = 3 * hidden_width
    both = dot(stacked(pieces, 0, cols), column(0, 2 * hidden_width), first_first).astype(BF16)
    gate_up[0] = both[:, :hidden_width]
    gate_up[1] = both[:, hidden_width:]
    down[...] = dot(
        column(2 * hidden_width, hidden_width), stacked(pieces, 1, cols), first_first
    ).astype(BF16)
    flight = (own_wide.shape[2] - core) // experts
    lg = jnp.concatenate(
        [
            w[j, :, core + f * experts : core + (f + 1) * experts]
            for w in (own_wide, twin_wide)
            for j in range(blocks)
            for f in range(flight)
        ]
    )
    router[...] = dot(stacked(pieces_all, 0, mine), lg, first_first).astype(BF16)


def pass_kernel(*refs):
    pass


def place_kernel(to_a, odd, block, last, _, out_a, out_b, mark, held, sem):
    tokens, width = held.shape
    step = width // 4
    order = order_of(last[:1, width:].astype(F32))
    for c in range(4):
        cols = slice(c * step, (c + 1) * step)
        rows = jnp.concatenate([last[:, cols], block[:, cols]])
        held[:, cols] = dot(order, rows, first_first).astype(BF16)
        for mine, out in ((to_a, out_a), (1 - to_a, out_b)):

            @pl.when(odd[0] == mine)
            def _(out=out, cols=cols):
                pltpu.make_async_copy(held.at[:, cols], out.at[:, cols], sem).start()

    mark[...] = jnp.zeros_like(mark)
    pltpu.make_async_copy(held, out_a, sem).wait()


def placed(to_a, odd, block, last, after):
    width = block.shape[1]
    tokens = block.shape[0] + last.shape[0]
    return call(
        functools.partial(place_kernel, to_a),
        [((tokens, width), BF16)] * 2 + [((8, 128), F32)],
        (odd, block, last, after),
        in_specs=[scalar] + [whole] * 3,
        out_specs=[outside] * 2 + [whole],
        scratch_shapes=[pltpu.VMEM((tokens, width), BF16), pltpu.SemaphoreType.DMA],
    )


def early_kernel(block, _, out, places):
    tokens, width = out.shape
    step = width // 4
    places[...] = jnp.broadcast_to(block[:1, width:].astype(F32), places.shape)
    order = order_of(places[:1, :])[tokens - block.shape[0] :]
    for c in range(4):
        cols = slice(c * step, (c + 1) * step)
        out[:, cols] = dot(order, block[:, cols], first_first).astype(BF16)


def finish_kernel(to_a, odd, early, places, last, *refs):
    outs, held, sem = refs[-4:-2], refs[-2], refs[-1]
    tokens, width = held.shape
    step = width // 8
    order = order_of(places[:1, :])[: last.shape[0]]
    for c in range(8):
        cols = slice(c * step, (c + 1) * step)
        late = dot(order, last[:, cols], first_first).astype(BF16)
        held[:, cols] = early[:, cols] + late
        for mine, out in ((to_a, outs[0]), (1 - to_a, outs[1])):

            @pl.when(odd[0] == mine)
            def _(out=out, cols=cols):
                pltpu.make_async_copy(held.at[:, cols], out.at[:, cols], sem).start()

    pltpu.make_async_copy(held, outs[0], sem).wait()


def placed_in_two(to_a, odd, block, last, before, after):
    slots, width = last.shape
    tokens = block.shape[0] + slots
    early, places = call(
        early_kernel,
        [((tokens, width), BF16), ((8, tokens), F32)],
        (block, after),
        in_specs=[whole] * 2,
        out_specs=[whole] * 2,
    )
    return call(
        functools.partial(finish_kernel, to_a),
        [((tokens, width), BF16)] * 2,
        (odd, early, places, last, *before),
        in_specs=[scalar] + [whole] * 3 + [outside] * 2,
        out_specs=[outside] * 2,
        scratch_shapes=[pltpu.VMEM((tokens, width), BF16), pltpu.SemaphoreType.DMA],
        input_output_aliases={4: 0, 5: 1},
    )


def on_device(section_in_a, route_a, router, gate_up, down_proj, section_in_b, route_b, grad_out_b):
    groups = lax.axis_size("expert")
    pipe = lax.axis_size("pipe")
    me = lax.axis_index("expert")
    wsplit = min(8, groups)
    flight = groups // wsplit
    mine = me // wsplit
    tok_rows, width = section_in_a.shape[1:]
    topk = route_a.shape[2]
    slot_count = tok_rows // 8
    slots = flight * slot_count
    router_table = router[0]
    experts = router_table.shape[1]
    hidden_width = gate_up.shape[3]
    bits = [1 << k for k in reversed(range(groups.bit_length() - 1))]

    odd = lax.axis_index("pipe") % 2
    sources = (route_b[0].T, route_a[0].T, section_in_b[0], grad_out_b[0], section_in_a[0])
    packed, twin_rows, sel_a, sel_b, first_near, first_far, at_near, at_far, to_near, to_far = call(
        functools.partial(pick_kernel, flight, slot_count, topk),
        [
            ((3, slots, width + experts), BF16),
            ((2, slots, width), BF16),
            ((slots, tok_rows), BF16),
            ((slots, tok_rows), BF16),
            ((slots, width), BF16),
            ((slots, width), BF16),
            ((slots, tok_rows), BF16),
            ((slots, tok_rows), BF16),
            ((tok_rows - slots, width + tok_rows), BF16),
            ((tok_rows - slots, width), BF16),
        ],
        (odd.reshape(1), *sources),
        limit=61,
        in_specs=[scalar] + [outside] * 5,
        out_specs=[whole] * 8 + [outside] * 2,
        scratch_shapes=[pltpu.VMEM((topk, tok_rows), jnp.int32)] * 2
        + [pltpu.VMEM((tok_rows, width), BF16)] * 3
        + [
            pltpu.VMEM((tok_rows - slots, width + tok_rows), BF16),
            pltpu.VMEM((tok_rows - slots, width), BF16),
        ]
        + [pltpu.SemaphoreType.DMA((7,))],
    )

    def everywhere(block):
        pieces = [block]
        for bit in bits:
            pieces += [exchanged(piece, bit) for piece in pieces]
        return pieces

    def of_mine(piece):
        if flight == 1:
            return piece
        split = piece.reshape(piece.shape[0], flight, slot_count, piece.shape[2])
        return lax.dynamic_index_in_dim(split, mine, axis=1, keepdims=False)

    def spread(values):
        if flight == 1:
            return values
        here = (jnp.arange(flight) == mine)[:, None, None]
        full = jnp.where(here, values[..., None, :, :], jnp.zeros((), values.dtype))
        return full.reshape(values.shape[:-2] + (slots, values.shape[-1]))

    own_all = everywhere(packed)
    from_near = lax.ppermute(to_near, "pipe", near(pipe))
    from_twin = lax.ppermute(twin_rows, "pipe", twins(pipe))
    (to_far,) = call(
        pass_kernel,
        [(to_far.shape, BF16)],
        (to_far, from_twin),
        in_specs=[outside, anywhere],
        out_specs=[outside],
        input_output_aliases={0: 0},
    )
    from_far = lax.ppermute(to_far, "pipe", far(pipe))
    twin_all = everywhere(from_twin)
    twin = [of_mine(p) for p in twin_all]
    own = [of_mine(p) for p in own_all]
    rows_all = groups * slot_count
    lanes = 2 * width + 128

    *parts, basis, factors = call(
        functools.partial(expert_kernel, groups, topk),
        [((slot_count, lanes), BF16)] * groups
        + [((groups, slot_count, experts), F32), ((rows_all, 3 * hidden_width), BF16)],
        (mine.reshape(1), *own, router_table, gate_up[0], down_proj[0]),
        limit=50,
        in_specs=[scalar] + [whole] * groups + [outside] * 3,
        out_specs=[whole] * (groups + 2),
        scratch_shapes=[
            pltpu.VMEM((2 * rows_all, width), BF16),
            pltpu.VMEM((rows_all, width), BF16),
            pltpu.VMEM((2 * rows_all, experts), F32),
            pltpu.VMEM((width, experts), BF16),
            pltpu.VMEM((2, width, hidden_width), BF16),
            pltpu.VMEM((hidden_width, width), BF16),
            pltpu.SemaphoreType.DMA((4,)),
        ],
    )
    if flight > 1:
        held = jnp.concatenate([piece[0] for piece in own_all]).reshape(groups * slots, -1)
        named = jnp.tile(jnp.repeat(jnp.arange(flight), slot_count), groups)
        basis = gates(
            held[:, width:].astype(F32),
            dot(held[:, :width], router_table),
            topk,
            named.astype(F32)[:, None],
        )[1].reshape(groups, slots, experts)
    terms = [[spread(part)] for part in parts]
    span, carrier = groups, terms[0][0]
    for bit in reversed(bits):
        sums = [terms[j][0] for j in range(span // 2, span)]
        split = span == 2
        if span < groups:
            sizes = [len(terms[j]) for j in range(span // 2, span)]
            given = [term for j in range(span // 2, span) for term in terms[j]]
            sums = call(
                functools.partial(middle_kernel, groups, span, sizes, split),
                [((slots, width), BF16), ((slots, width + 128), BF16)]
                if split
                else [((slots, lanes), BF16)] * len(sizes),
                (carrier, terms[span - 1][-1], *given, *twin_all),
                in_specs=[whole] * (2 + len(given)) + [anywhere] * groups,
                out_specs=[whole] * (2 if split else len(sizes)),
            )
            carrier = sums[-1]
        span //= 2
        if split:
            terms[0] += [exchanged(value, bit) for value in sums]
        else:
            for j in reversed(range(span)):
                terms[j].append(exchanged(sums[j], bit))
    last_near, last_far, wide = call(
        functools.partial(last_kernel, groups, span, len(terms[0])),
        [
            ((slots, width), BF16),
            ((slots, width + tok_rows), BF16),
            ((groups, slot_count, 3 * hidden_width + flight * experts), BF16),
        ],
        (
            odd.reshape(1),
            carrier,
            *terms[0],
            basis,
            router_table,
            factors,
            sel_a,
            sel_b,
            first_near,
            first_far,
            at_near,
            at_far,
        ),
        in_specs=[scalar] + [whole] * (len(terms[0]) + 10),
        out_specs=[whole] * 3,
    )
    twin_wide = lax.ppermute(wide, "pipe", twins(pipe))
    last_near = lax.ppermute(last_near, "pipe", near(pipe))
    last_far = lax.ppermute(last_far, "pipe", far(pipe))

    share = width // groups
    tiles = min(8, share // 128)
    tile = width // tiles
    same = flight == 1
    held = (*own, *twin) if same else (*own, *twin, *own_all, *twin_all)
    grad_gate_up, grad_down, grad_router, mark = call(
        functools.partial(grads_kernel, groups, hidden_width, experts, same),
        [
            ((2, width, hidden_width), BF16),
            ((hidden_width, width), BF16),
            ((share, experts), BF16),
            ((8, 128), F32),
        ],
        (me.reshape(1), *held, wide, twin_wide),
        grid=(tiles,),
        in_specs=[scalar] + [whole] * (len(held) + 2),
        out_specs=[
            pl.BlockSpec((2, tile, hidden_width), lambda i: (0, i, 0)),
            pl.BlockSpec((hidden_width, tile), lambda i: (0, i)),
            pl.BlockSpec((share // tiles, experts), lambda i: (i, 0)),
            pl.BlockSpec((8, 128), lambda i: (0, 0)),
        ],
    )
    odd = odd.reshape(1)
    *outs, mark = placed(0, odd, from_far, last_far, mark)
    section_out_a, grad_in_b = placed_in_two(1, odd, from_near, last_near, outs, mark)
    return (
        section_out_a[None],
        grad_in_b[None],
        grad_gate_up[None],
        grad_down[None],
        grad_router[None],
    )


def solution(mesh):
    return jax.shard_map(
        on_device,
        mesh=mesh,
        in_specs=(
            P("pipe", "expert", None),
            P("pipe", "expert", None),
            P("pipe", None, None),
            P("pipe", None, None, "expert"),
            P("pipe", "expert", None),
            P("pipe", "expert", None),
            P("pipe", "expert", None),
            P("pipe", "expert", None),
        ),
        out_specs=(
            P("pipe", "expert", None),
            P("pipe", "expert", None),
            P("pipe", None, None, "expert"),
            P("pipe", "expert", None),
            P("pipe", "expert", None),
        ),
        check_vma=False,
    )
```
